128 devices in a mesh: row: 8 (over x, core), col: 16 (over y, z).
Axes of the slice: x: 4, y: 4, z: 4, core: 2. Of those that a mesh axis runs over, the one named last changes fastest.
Arguments:
- leaf_source: float32 [2, 128, 1024, 256], P(None, ('row', 'col')), may hold values from -6 to 6
- leaf_inv: float32 [128, 2, 512, 512], P(('row', 'col')), as said below
- leaf_low: float32 [128, 2, 512, 512], P(('row', 'col')), may hold values from -0.1875 to 0.1875
- child_count: int32 [128], replicated, may hold values from 256 to 512
- child_owner: int32 [128, 512, 1], replicated, may hold values from 0 to 127; in each aligned block of 512 rows (0 to 511, 512 to 1023, ..., all dimensions but the last counted through in order) at most 6 rows name the same one
- child_slot: int32 [128, 512], replicated, may hold values from 0 to 127
- parent_source: float32 [2, 16384, 256], P(None, ('row', 'col')), may hold values from -6 to 6
- parent_inv: float32 [2, 16384, 16384], P(None, 'row', 'col'), as said below
- kernel_coef: float32 [3, 16384], P(None, ('row', 'col')), may hold values from 0.5 to 2
- p_speed: float32 [16384], P(('row', 'col')), may hold values from 1 to 2
- s_speed: float32 [16384], P(('row', 'col')), may hold values from 0.4 to 0.8
- density: float32 [16384], P(('row', 'col')), may hold values from 0.8 to 1.2
Outputs:
- gradient: float32 [3, 16384], P(None, ('row', 'col'))
The draws below stay inside these ranges and needn't reach their ends.
Inputs may be any that keep to these rules, and one draw needn't show every extreme that they name: `child_owner`: in each aligned block of 512 rows (one child's rows) no owner appears more than 6 times, and some owner appears exactly 6 times. `leaf_inv`: each child's matrix is unit lower triangular: real part 1 and imaginary part 0 on the diagonal, zero above. `parent_inv`: lower triangular in elimination order: stored row p maps to elimination row ((l div 64) * 8 + r) * 64 + l mod 64 with r = p div (2048), l = p mod (2048); stored columns likewise with 16; the diagonal is 1 (real), entries above it zero.
All inputs are finite; a program needn't handle non-finite values.
Results may differ from the reference program's by a relative error of at most 0.00029.
Values sent between devices are 32-bit elements; how exact they have to be, the bound alone decides.
No kernel may reach another device: no remote copies, remote signals or barrier semaphores. Data moves between devices by JAX's collectives and lax.ppermute only.
A program may use at most 128 MiB of HBM per device.

```python
import math
import jax
import jax.numpy as jnp
import numpy as np
from jax import lax

PIVOT = 512
CONTRIB = 512
FRONT = 16384
BLOCK = 64
SOURCES = 128
OWNED = 128
CAPACITY = 6
N_ROW = 8
N_COL = 16
DEVICES = 128


def draw_leaf_inv(key, part):
    key = jax.random.fold_in(key, 5)
    values = jax.random.normal(key, (DEVICES, 2, PIVOT, PIVOT), jnp.float32)
    values = values / jnp.sqrt(jnp.float32(PIVOT))
    position = jnp.arange(PIVOT)
    lower = position[:, None] > position[None, :]
    diagonal = (position[:, None] == position[None, :]).astype(jnp.float32)
    real_part = jnp.where(lower, values[:, 0], diagonal)
    imag_part = jnp.where(lower, values[:, 1], 0.0)
    return jnp.stack([real_part, imag_part], axis=1)


def elimination_order(count_parts):
    stored = jnp.arange(FRONT)
    per_part = FRONT // count_parts
    owner_part = stored // per_part
    within = stored % per_part
    return (within // BLOCK * count_parts + owner_part) * BLOCK + within % BLOCK


def draw_parent_inv(key, part):
    key = jax.random.fold_in(key, 11)
    values = jax.random.normal(key, (2, FRONT, FRONT), jnp.float32)
    values = values / jnp.sqrt(jnp.float32(FRONT))
    row_order = elimination_order(N_ROW)
    col_order = elimination_order(N_COL)
    lower = row_order[:, None] > col_order[None, :]
    diagonal = (row_order[:, None] == col_order[None, :]).astype(jnp.float32)
    real_part = jnp.where(lower, values[0], diagonal)
    imag_part = jnp.where(lower, values[1], 0.0)
    return jnp.stack([real_part, imag_part])


def plant(drawn, stream_key, low, high):
    shape = drawn.shape
    index_at = [jax.random.randint(jax.random.fold_in(stream_key, axis), (), 0, shape[axis]) for axis in range(len(shape))]
    drawn = drawn.at[tuple(index_at)].set(low)
    longest = shape.index(max(shape))
    index_at[longest] = (index_at[longest] + 1) % shape[longest]
    return drawn.at[tuple(index_at)].set(high)


def steps_of(stream_key, shape, split, least, largest):
    loudness = 1.0
    for axis_at, shards_of in split:
        heights = jax.random.uniform(jax.random.fold_in(jax.random.fold_in(stream_key, 6), axis_at), (shards_of,), jnp.float32, least / len(split), largest / len(split))
        loudness = loudness * jnp.repeat(jnp.exp(heights), shape[axis_at] // shards_of).reshape((-1,) + (1,) * (len(shape) - 1 - axis_at))
    return loudness


def shared_out(rng, own, number, rows, number_of, top, most, skew):
    sequence = jax.random.permutation(rng, number_of)
    crowded, ordinary = shares(number_of, rows * top, most, skew, True), shares(number_of, rows * top, most, skew, False)
    places = jnp.arange(number_of)

    def named(sizes, turn):
        used = int((sizes > 0).sum())
        fixed = max(1, used // 4)
        passed = fixed + (places - fixed + turn * (used - fixed)) % max(1, number_of - fixed)
        return jnp.zeros((number_of,), jnp.int32).at[sequence[jnp.where(places < fixed, places, passed)]].set(jnp.asarray(sizes, jnp.int32))

    sizes = jnp.where(number % 4 == 0, named(crowded, number // 4), named(ordinary, number - number // 4 - 1))
    mixed = jax.random.permutation(jax.random.fold_in(own, 3), number_of)
    donor, receiver = mixed[0:number_of // 2 * 2:2], mixed[1:number_of // 2 * 2:2]
    room = jnp.minimum(sizes[donor] - 1, most - sizes[receiver]) // 2
    room = jnp.where((donor == sequence[0]) | (receiver == sequence[0]) | (sizes[receiver] == 0), 0, jnp.maximum(room, 0))
    passed = jax.random.randint(jax.random.fold_in(own, 4), (number_of // 2,), 0, 1 << 20) % (room + 1)
    sizes = sizes.at[donor].add(-passed).at[receiver].add(passed)
    items = jnp.searchsorted(jnp.cumsum(sizes), jnp.arange(rows * top), side="right").astype(jnp.int32)
    table = items.reshape(top, rows).T
    table = table[jax.random.permutation(jax.random.fold_in(own, 1), rows)]
    turn = jax.random.randint(jax.random.fold_in(own, 2), (rows, 1), 0, top)
    return jnp.take_along_axis(table, (jnp.arange(top)[None, :] + turn) % top, axis=1)


def shares(count, total, bound, slope, full):
    weights = [(1 << 20) // math.isqrt(rank ** slope) + 1 for rank in range(1, count + 1)]
    largest = bound if full else min(bound, max(-(-total // count), total * weights[0] // sum(weights)))
    least = 1 if total - largest >= count - 1 else 0
    given, surplus = [largest] + [least] * (count - 1), total - largest - least * (count - 1)
    while surplus > 0:
        movable = [i for i in range(1, count) if given[i] < largest] or [i for i in range(1, count) if given[i] < bound]
        mass, budget = sum([weights[i] for i in movable]), surplus
        for i in movable:
            addition = min(bound - given[i], max(1, budget * weights[i] // mass), surplus)
            given[i] = given[i] + addition
            surplus = surplus - addition
    return np.array(given)


def gaussian(rng, shape, deviation, limit, split=(), kind=jnp.bfloat16):
    result = deviation * jax.random.normal(rng, shape, jnp.float32)
    if split:
        result = result * steps_of(rng, shape, split, -0.22, 0.18)
    return jnp.clip(result, -limit, limit).astype(kind)


def setup_inputs(seed: int = 0) -> dict:
    seeds = jax.random.split(jax.random.key(seed), 13)
    leaf_source = gaussian(seeds[0], (2, DEVICES, PIVOT + CONTRIB, 2 * SOURCES), 1.0, 6.0, ((1, 128),), jnp.float32)
    leaf_inv = draw_leaf_inv(jax.random.fold_in(seeds[12], 71), 0)
    leaf_low = gaussian(seeds[2], (DEVICES, 2, CONTRIB, PIVOT), (2 * PIVOT) ** -0.5, 0.1875, ((0, 128),), jnp.float32)
    child_count = plant(jax.random.randint(seeds[3], (DEVICES,), CONTRIB // 2, CONTRIB + 1), jax.random.fold_in(seeds[3], 1), CONTRIB // 2, CONTRIB).astype(jnp.int32)
    child_owner_keys = jax.random.split(jax.random.fold_in(seeds[4], 1), DEVICES * CONTRIB // CONTRIB)
    child_owner_turns = jax.random.permutation(jax.random.fold_in(seeds[4], 3), DEVICES * CONTRIB // CONTRIB)
    child_owner = jax.vmap(lambda own, number: shared_out(jax.random.fold_in(seeds[4], 2), own, number, CONTRIB, DEVICES, 1, CAPACITY, 2))(child_owner_keys, child_owner_turns).reshape((DEVICES, CONTRIB, 1))
    child_slot = plant(jax.random.randint(seeds[5], (DEVICES, CONTRIB), 0, OWNED), jax.random.fold_in(seeds[5], 1), 0, OWNED - 1).astype(jnp.int32)
    parent_source = gaussian(seeds[6], (2, FRONT, 2 * SOURCES), 1.0, 6.0, ((1, 128),), jnp.float32)
    parent_inv = draw_parent_inv(jax.random.fold_in(seeds[12], 71), 0)
    kernel_coef = jnp.clip(jnp.exp(math.log(2.0) - 1.3862944 * jax.random.uniform(seeds[8], (3, FRONT), jnp.float32) ** steps_of(seeds[8], (3, FRONT), ((1, 128),), -0.2, 0.2)), 0.5, 2.0)
    p_speed = jnp.clip(1.0 + 1.0 * jax.random.uniform(seeds[9], (FRONT,), jnp.float32) ** steps_of(seeds[9], (FRONT,), ((0, 128),), -0.2, 0.2), 1.0, 2.0)
    s_speed = jnp.clip(0.4 + 0.4 * jax.random.uniform(seeds[10], (FRONT,), jnp.float32) ** steps_of(seeds[10], (FRONT,), ((0, 128),), -0.2, 0.2), 0.4, 0.8)
    density = jnp.clip(0.8 + 0.40000004 * jax.random.uniform(seeds[11], (FRONT,), jnp.float32) ** steps_of(seeds[11], (FRONT,), ((0, 128),), -0.2, 0.2), 0.8, 1.2)
    return {"leaf_source": leaf_source, "leaf_inv": leaf_inv, "leaf_low": leaf_low, "child_count": child_count, "child_owner": child_owner, "child_slot": child_slot, "parent_source": parent_source, "parent_inv": parent_inv, "kernel_coef": kernel_coef, "p_speed": p_speed, "s_speed": s_speed, "density": density}


HIGHEST = lax.Precision.HIGHEST

def complex_product(former, latter):

    def single(left_op, right_op):
        return jnp.dot(left_op, right_op, preferred_element_type=jnp.float32, precision=HIGHEST)
    real_part = single(former[0], latter[0]) - single(former[1], latter[1])
    imag_part = single(former[0], latter[1]) + single(former[1], latter[0])
    return jnp.stack([real_part, imag_part])

def material_gradient(eliminated, kernel_coef, p_speed, s_speed, density):
    norming = 1.0 / jnp.sqrt(jnp.float32(SOURCES))
    fwd_real = eliminated[0, :, :SOURCES]
    fwd_imag = eliminated[1, :, :SOURCES]
    adj_real = eliminated[0, :, SOURCES:]
    adj_imag = eliminated[1, :, SOURCES:]
    k_lambda = lax.optimization_barrier(jnp.sum(fwd_real * adj_real - fwd_imag * adj_imag, axis=1)) * norming
    k_mu = lax.optimization_barrier(jnp.sum(fwd_real * adj_imag + fwd_imag * adj_real, axis=1)) * norming
    k_rho = lax.optimization_barrier(jnp.sum(fwd_real * adj_real + fwd_imag * adj_imag, axis=1)) * norming
    grad_lambda = kernel_coef[0] * k_lambda
    grad_mu = kernel_coef[1] * k_mu
    grad_rho = kernel_coef[2] * k_rho
    first_out = 2.0 * density * p_speed * grad_lambda
    second_out = 2.0 * density * s_speed * (grad_mu - 2.0 * grad_lambda)
    third_out = (p_speed * p_speed - 2.0 * s_speed * s_speed) * grad_lambda + s_speed * s_speed * grad_mu + grad_rho
    return jnp.stack([first_out, second_out, third_out])

def reference(leaf_source, leaf_inv, leaf_low, child_count, child_owner, child_slot, parent_source, parent_inv, kernel_coef, p_speed, s_speed, density):

    def leaf_solve(operands):
        source_part, inverse_part, lower_part = operands
        pivot_part = complex_product(inverse_part, source_part[:, :PIVOT])
        return source_part[:, PIVOT:] - complex_product(lower_part, pivot_part)
    moved = jnp.moveaxis(leaf_source, 1, 0)
    updates = lax.map(leaf_solve, (moved, leaf_inv, leaf_low))
    live = (jnp.arange(CONTRIB, dtype=jnp.int32)[None, :] < child_count[:, None]).astype(jnp.float32)
    updates = updates * live[:, None, :, None]
    owners = child_owner[:, :, 0]
    target = owners % N_COL * (FRONT // N_COL) + owners // N_COL * OWNED + child_slot
    target = target.astype(jnp.int32)
    front_rows = jnp.arange(FRONT, dtype=jnp.int32)
    holder = front_rows // OWNED
    from_row = (holder % N_ROW * N_COL + holder // N_ROW) * OWNED + front_rows % OWNED
    arranged = parent_source[:, from_row.astype(jnp.int32)]
    flat_rows = jnp.transpose(updates, (1, 0, 2, 3)).reshape(2, DEVICES * CONTRIB, 2 * SOURCES)
    assembled = arranged.at[:, target.reshape(-1)].add(flat_rows)
    eliminated = complex_product(parent_inv, assembled)
    return material_gradient(eliminated, kernel_coef, p_speed, s_speed, density)
```

```python
import functools

import jax
import jax.numpy as jnp
from jax import lax
from jax.experimental import pallas as pl
from jax.experimental.pallas import tpu as pltpu
from jax.sharding import PartitionSpec as P

SOURCES = 128
CAPACITY = 6
LANES = 128
RING = 4
F32 = jnp.float32
BF16 = jnp.bfloat16


def halves(value):
    high = value.astype(BF16)
    return high, (value - high.astype(F32)).astype(BF16)


def dot(left, right, dims=((1,), (0,))):
    return lax.dot_general(left, right, (dims, ((), ())), preferred_element_type=F32)


def dot3(left, right_high, right_low):
    left_high, left_low = halves(left)
    return dot(left_high, right_high) + (dot(left_high, right_low) + dot(left_low, right_high))


def complex_rows(real_left, imag_left, right):
    breadth = right.shape[1] // 2
    high, low = halves(right)
    by_real = dot3(real_left, high, low)
    by_imag = dot3(imag_left, high, low)
    real_part = by_real[:, :breadth] - by_imag[:, breadth:]
    imag_part = by_real[:, breadth:] + by_imag[:, :breadth]
    return real_part, imag_part


def running_count(mask):
    length = mask.shape[1]
    former = lax.broadcasted_iota(jnp.int32, (length, length), 0)
    latter = lax.broadcasted_iota(jnp.int32, (length, length), 1)
    upto = jnp.where(former <= latter, 1.0, 0.0).astype(BF16)
    return dot(mask.astype(BF16), upto)


def leaf_kernel(place, owner_ref, source_ref, inv_ref, low_ref, out_ref):
    pivots = inv_ref.shape[1]
    devices = owner_ref.shape[0]
    contrib = owner_ref.shape[1]
    pivot_source = jnp.concatenate([source_ref[0, :pivots], source_ref[1, :pivots]], axis=1)
    pivot_part = jnp.concatenate(complex_rows(inv_ref[0], inv_ref[1], pivot_source), axis=1)
    real_low, imag_low = complex_rows(low_ref[0], low_ref[1], pivot_part)
    update = jnp.concatenate(
        [source_ref[0, pivots:] - real_low, source_ref[1, pivots:] - imag_low], axis=1
    )
    high, low = halves(update)
    my_owner = owner_ref[pl.ds(place[0], 1), :]
    names = lax.broadcasted_iota(jnp.int32, (devices, contrib), 0)
    chosen = jnp.where(names == my_owner, 1.0, 0.0)
    rank = running_count(chosen) * chosen
    groups = update.shape[1] // LANES
    for k in range(CAPACITY):
        pick = jnp.where(rank == k + 1.0, 1.0, 0.0).astype(BF16)
        rows = dot(pick, high) + dot(pick, low)
        for g in range(groups):
            out_ref[pl.ds(k * groups + g, devices, stride=CAPACITY * groups), :] = rows[
                :, g * LANES : (g + 1) * LANES
            ]


def placing_kernel(place, owner_ref, slot_ref, out_ref):
    devices = owner_ref.shape[0]
    owned = out_ref.shape[2]
    mine = jnp.where(owner_ref[...] == place[0], 1.0, 0.0)
    rank = running_count(mine) * mine
    slots = slot_ref[...].astype(F32) + 1.0
    rows = lax.broadcasted_iota(jnp.int32, (devices, owned), 1).astype(F32) + 1.0
    for k in range(CAPACITY):
        slot = jnp.sum(jnp.where(rank == k + 1.0, slots, 0.0), axis=1, keepdims=True)
        out_ref[k] = jnp.where(slot == rows, 1.0, 0.0).astype(BF16)


def extend_kernel(placing_ref, arrived_ref, parent_ref, out_ref):
    devices = placing_ref.shape[1]
    groups = out_ref.shape[1] // LANES
    breadth = parent_ref.shape[2]
    for g in range(groups):
        at = g * LANES
        total = parent_ref[at // breadth, :, at % breadth : at % breadth + LANES]
        for k in range(CAPACITY):
            rows = arrived_ref[pl.ds(k * groups + g, devices, stride=CAPACITY * groups), :]
            high, low = halves(rows)
            total += dot(placing_ref[k], high, ((0,), (0,)))
            total += dot(placing_ref[k], low, ((0,), (0,)))
        out_ref[:, at : at + LANES] = total


def parent_kernel(place, inv_ref, own_ref, other_ref, left_ref, right_ref, far_ref, swapped_ref, *rest):
    along_y, along_z, (high_ref, low_ref) = rest[:RING], rest[RING : 2 * RING], rest[2 * RING :]
    step = pl.program_id(0)
    owned, width = own_ref.shape
    breadth = width // 2
    depth = 2 * owned
    block = inv_ref.shape[1]
    own_x, own_core, own_y, own_z = place[1], place[2], place[3], place[4]

    @pl.when(step == 0)
    def _():
        def fill(value, from_x, core):
            at = pl.multiple_of((lax.rem(from_x + RING, RING) * 2 + core) * owned, owned)
            high, low = halves(value)
            high_ref[pl.ds(at, owned), :] = high
            low_ref[pl.ds(at, owned), :] = low

        fill(own_ref[...], own_x, own_core)
        fill(other_ref[...], own_x, 1 - own_core)
        for at, (hop, ref) in enumerate(((1, left_ref), (3, right_ref), (2, far_ref))):
            fill(ref[...], own_x - hop, own_core)
            fill(swapped_ref[at], own_x - hop, 1 - own_core)

    def finish(total_real, total_imag):
        for j in range(block // owned):
            column = step * (block // owned) + j
            hop_y = lax.rem(column // RING - own_y + RING, RING)
            hop_z = lax.rem(lax.rem(column, RING) - own_z + RING, RING)
            rows = slice(j * owned, (j + 1) * owned)
            real_part, imag_part = total_real[rows], total_imag[rows]
            forward = jnp.concatenate([real_part[:, :SOURCES], imag_part[:, :SOURCES]], axis=1)
            adjoint = jnp.concatenate([real_part[:, SOURCES:], imag_part[:, SOURCES:]], axis=1)
            for hop in range(RING):

                @pl.when(hop_y == hop)
                def _(hop=hop):
                    along_y[hop][hop_z] = forward

                @pl.when(hop_z == hop)
                def _(hop=hop):
                    along_z[hop][hop_y] = adjoint

    pieces = inv_ref.shape[2] // depth
    for reach in range(pieces):

        @pl.when(step * block // (2 * depth) == reach)
        def _(reach=reach):
            deep = (reach + 1) * depth
            high, low = high_ref[:deep], low_ref[:deep]
            by_real = dot3(inv_ref[0, :, :deep], high, low)
            by_imag = dot3(inv_ref[1, :, :deep], high, low)
            finish(
                by_real[:, :breadth] - by_imag[:, breadth:],
                by_real[:, breadth:] + by_imag[:, :breadth],
            )


def material_gradient(forward, adjoint, kernel_coef, p_speed, s_speed, density):
    norming = 1.0 / jnp.sqrt(jnp.float32(SOURCES))
    fwd_real, fwd_imag = forward[:, :SOURCES], forward[:, SOURCES:]
    adj_real, adj_imag = adjoint[:, :SOURCES], adjoint[:, SOURCES:]
    k_lambda = jnp.sum(fwd_real * adj_real - fwd_imag * adj_imag, axis=1) * norming
    k_mu = jnp.sum(fwd_real * adj_imag + fwd_imag * adj_real, axis=1) * norming
    k_rho = jnp.sum(fwd_real * adj_real + fwd_imag * adj_imag, axis=1) * norming
    grad_lambda = kernel_coef[0] * k_lambda
    grad_mu = kernel_coef[1] * k_mu
    grad_rho = kernel_coef[2] * k_rho
    first_out = 2.0 * density * p_speed * grad_lambda
    second_out = 2.0 * density * s_speed * (grad_mu - 2.0 * grad_lambda)
    third_out = (
        (p_speed * p_speed - 2.0 * s_speed * s_speed) * grad_lambda
        + s_speed * s_speed * grad_mu
        + grad_rho
    )
    return jnp.stack([first_out, second_out, third_out])


def along(axis, hop):
    if axis == "core":
        return [(i, i ^ 1) for i in range(2 * RING)]
    if axis == "x":
        return [(i, (i + 2 * hop) % (2 * RING)) for i in range(2 * RING)]
    if axis == "y":
        return [(i, (i + RING * hop) % (RING * RING)) for i in range(RING * RING)]
    return [(i, i // RING * RING + (i + hop) % RING) for i in range(RING * RING)]


def move(value, axis, hop=1):
    return lax.ppermute(value, "row" if axis in ("x", "core") else "col", along(axis, hop))


def params(mebibytes, **more):
    return pltpu.CompilerParams(vmem_limit_bytes=mebibytes << 20, **more)


SMEM = pl.BlockSpec(memory_space=pltpu.SMEM)
VMEM = pl.BlockSpec(memory_space=pltpu.VMEM)


def per_device(
    leaf_source,
    leaf_inv,
    leaf_low,
    child_count,
    child_owner,
    child_slot,
    parent_source,
    parent_inv,
    kernel_coef,
    p_speed,
    s_speed,
    density,
):
    row, col = lax.axis_index("row"), lax.axis_index("col")
    devices = lax.axis_size("row") * lax.axis_size("col")
    owned = parent_source.shape[1]
    width = 2 * parent_source.shape[2]
    place = jnp.stack([row * lax.axis_size("col") + col, row // 2, row % 2, col // RING, col % RING])
    position = jnp.arange(child_slot.shape[1], dtype=jnp.int32)
    owner = jnp.where(position[None, :] < child_count[:, None], child_owner[:, :, 0], -1)

    outgoing = pl.pallas_call(
        leaf_kernel,
        out_shape=jax.ShapeDtypeStruct((devices * CAPACITY * width // LANES, LANES), F32),
        in_specs=[SMEM] + [VMEM] * 4,
        out_specs=VMEM,
        compiler_params=params(40),
        name="leaf",
    )(place, owner, leaf_source[:, 0], leaf_inv[0], leaf_low[0])
    placing = pl.pallas_call(
        placing_kernel,
        out_shape=jax.ShapeDtypeStruct((CAPACITY, devices, owned), BF16),
        in_specs=[SMEM] + [VMEM] * 2,
        out_specs=VMEM,
        compiler_params=params(16),
        cost_estimate=pl.CostEstimate(flops=2 * devices * 512 * 512, bytes_accessed=1 << 20, transcendentals=0),
        name="placing",
    )(place, owner, child_slot)
    arrived = lax.all_to_all(
        outgoing.reshape(devices, -1, LANES), ("row", "col"), split_axis=0, concat_axis=0, tiled=True
    )
    assembled = pl.pallas_call(
        extend_kernel,
        out_shape=jax.ShapeDtypeStruct((owned, width), F32),
        in_specs=[VMEM] * 3,
        out_specs=VMEM,
        compiler_params=params(16),
        name="extend",
    )(placing, arrived.reshape(outgoing.shape), parent_source)

    other = move(assembled, "core")
    hops = [move(assembled, "x", hop) for hop in (1, 3, 2)]
    swapped = move(jnp.stack(hops), "core")

    block = 2 * owned
    steps = parent_inv.shape[1] // block
    piece = jax.ShapeDtypeStruct((RING, owned, width // 2), F32)
    whole = pl.BlockSpec((RING, owned, width // 2), lambda i: (0, 0, 0))
    part = pl.BlockSpec((owned, width), lambda i: (0, 0))
    sums = pl.pallas_call(
        parent_kernel,
        out_shape=[piece] * (2 * RING),
        grid=(steps,),
        in_specs=[
            SMEM,
            pl.BlockSpec((2, block, parent_inv.shape[2]), lambda i: (0, i, 0)),
            part, part, part, part, part,
            pl.BlockSpec((3, owned, width), lambda i: (0, 0, 0)),
        ],
        out_specs=[whole] * (2 * RING),
        scratch_shapes=[pltpu.VMEM((parent_inv.shape[2], width), BF16)] * 2,
        compiler_params=params(48),
        name="parent",
    )(place, parent_inv, assembled, other, *hops, swapped)
    along_y, along_z = sums[:RING], sums[RING:]

    hop_order = (1, 3, 2)
    from_y = [move(along_y[hop], "y", hop) for hop in hop_order]
    from_z = [move(along_z[hop], "z", hop) for hop in hop_order]
    plane_y = along_y[0] + from_y[0] + from_y[1] + from_y[2]
    plane_z = along_z[0] + from_z[0] + from_z[1] + from_z[2]
    then_z = [move(plane_y[hop], "z", hop) for hop in hop_order]
    then_y = [move(plane_z[hop], "y", hop) for hop in hop_order]
    forward = plane_y[0] + then_z[0] + then_z[1] + then_z[2]
    adjoint = plane_z[0] + then_y[0] + then_y[1] + then_y[2]
    return material_gradient(forward, adjoint, kernel_coef, p_speed, s_speed, density)


def solution(mesh):
    return jax.shard_map(
        per_device,
        mesh=mesh,
        in_specs=(
            P(None, ("row", "col"), None, None),
            P(("row", "col"), None, None, None),
            P(("row", "col"), None, None, None),
            P(),
            P(),
            P(),
            P(None, ("row", "col"), None),
            P(None, "row", "col"),
            P(None, ("row", "col")),
            P(("row", "col")),
            P(("row", "col")),
            P(("row", "col")),
        ),
        out_specs=P(None, ("row", "col")),
        check_vma=False,
    )
```

```python
import functools

import jax
import jax.numpy as jnp
from jax import lax
from jax.experimental import pallas as pl
from jax.experimental.pallas import tpu as pltpu
from jax.sharding import PartitionSpec as P

SOURCES = 128
CAPACITY = 6
LANES = 128
RING = 4
F32 = jnp.float32
BF16 = jnp.bfloat16


def halves(value):
    high = value.astype(BF16)
    return high, (value - high.astype(F32)).astype(BF16)


def dot(left, right, dims=((1,), (0,))):
    return lax.dot_general(left, right, (dims, ((), ())), preferred_element_type=F32)


def left_parts(real_part, imag_part):
    real_high, real_low = halves(real_part)
    imag_high, imag_low = halves(imag_part)
    return jnp.concatenate([real_high, imag_high, real_high, imag_high, real_low, imag_low], axis=1)


def turned(value, part_width):
    parts = [value[:, at : at + part_width] for at in range(0, value.shape[1], part_width)]
    return jnp.concatenate(
        [part for at in range(0, len(parts), 2) for part in (-parts[at + 1], parts[at])], axis=1
    )


def right_parts(value):
    high, low = halves(value)
    turned_high, turned_low = (turned(part, value.shape[1] // 2) for part in (high, low))
    return jnp.concatenate([high, turned_high, low, turned_low, high, turned_high], axis=0)


def running_count(mask):
    length = mask.shape[1]
    former = lax.broadcasted_iota(jnp.int32, (length, length), 0)
    latter = lax.broadcasted_iota(jnp.int32, (length, length), 1)
    upto = jnp.where(former <= latter, 1.0, 0.0).astype(BF16)
    return dot(mask.astype(BF16), upto)


def leaf_kernel(
    place, count_ref, owner_hbm, source_hbm, inv_hbm, low_hbm, out_ref, owner_ref, source_ref, inv_ref, low_ref, sems
):
    devices, contrib = owner_hbm.shape[0], owner_ref.shape[1]
    pivots, breadth = inv_ref.shape[1], source_ref.shape[2]
    groups = 2 * breadth // LANES
    copies = [
        pltpu.make_async_copy(former, latter, sems.at[i])
        for i, (former, latter) in enumerate(
            (
                (source_hbm, source_ref),
                (inv_hbm, inv_ref),
                (owner_hbm.at[place[0]], owner_ref),
                (low_hbm, low_ref),
            )
        )
    ]
    for copy in copies:
        copy.start()
    copies[2].wait()
    names = lax.broadcasted_iota(jnp.int32, (devices, contrib), 0)
    position = lax.broadcasted_iota(jnp.int32, (devices, contrib), 1)
    chosen = jnp.where((names == owner_ref[...]) & (position < count_ref[place[0]]), 1.0, 0.0)
    rank = running_count(chosen) * chosen
    pick = jnp.concatenate(
        [jnp.where(rank == k + 1.0, 1.0, 0.0).astype(BF16) for k in range(CAPACITY)], axis=0
    )
    copies[0].wait()
    pivot_source = jnp.concatenate([source_ref[0, :pivots], source_ref[1, :pivots]], axis=1)
    copies[1].wait()
    half = pivots // 2
    upper = dot(
        left_parts(inv_ref[0, :half, :half], inv_ref[1, :half, :half]), right_parts(pivot_source[:half])
    )
    lower = dot(left_parts(inv_ref[0, half:], inv_ref[1, half:]), right_parts(pivot_source))
    pivot_part = jnp.concatenate([upper, lower], axis=0)
    copies[3].wait()
    eliminated = dot(left_parts(low_ref[0], low_ref[1]), right_parts(pivot_part))
    update = jnp.concatenate([source_ref[0, pivots:], source_ref[1, pivots:]], axis=1) - eliminated
    high, low = halves(update)
    rows = dot(jnp.concatenate([pick, pick], axis=1), jnp.concatenate([high, low], axis=0))
    for k in range(CAPACITY):
        for g in range(groups):
            at = (g % 2) * breadth + g // 2 * LANES
            out_ref[pl.ds(k * groups + g, devices, stride=CAPACITY * groups), :] = rows[
                k * devices : (k + 1) * devices, at : at + LANES
            ]


def placing_kernel(place, owner_ref, slot_ref, token_hbm, out_ref):
    del token_hbm
    devices = owner_ref.shape[0]
    owned = out_ref.shape[2]
    mine = jnp.where(owner_ref[...] == place[0], 1.0, 0.0)
    rank = running_count(mine) * mine
    slots = slot_ref[...].astype(F32) + 1.0
    rows = lax.broadcasted_iota(jnp.int32, (devices, owned), 1).astype(F32) + 1.0
    for k in range(CAPACITY):
        slot = jnp.sum(jnp.where(rank == k + 1.0, slots, 0.0), axis=1, keepdims=True)
        out_ref[k] = jnp.where(slot == rows, 1.0, 0.0).astype(BF16)


def extend_kernel(placing_ref, arrived_ref, parent_ref, out_ref):
    devices = placing_ref.shape[1]
    groups = out_ref.shape[1] // LANES
    for g in range(groups):
        total = parent_ref[g % 2, :, g // 2 * LANES : (g // 2 + 1) * LANES]
        for k in range(CAPACITY):
            rows = arrived_ref[pl.ds(k * groups + g, devices, stride=CAPACITY * groups), :]
            high, low = halves(rows)
            total += dot(placing_ref[k], high, ((0,), (0,)))
            total += dot(placing_ref[k], low, ((0,), (0,)))
        out_ref[:, g * LANES : (g + 1) * LANES] = total


def split_kernel(value_ref, after_hbm, high_ref, low_ref, token_ref):
    del after_hbm
    token_ref[...] = jnp.zeros_like(token_ref)
    step = pl.program_id(0)
    depth = value_ref.shape[2] // RING
    per_band = pl.num_programs(0) // RING
    for piece in range(RING):

        @pl.when(step // per_band >= piece)
        def _(piece=piece):
            columns = slice(piece * depth, (piece + 1) * depth)
            high_ref[:, :, columns], low_ref[:, :, columns] = halves(value_ref[:, :, columns])


def band_product(held, right_ref, band, blocks):
    deep = (band + 1) * 2 * held.shape[4]

    def rows(kind, part):
        return jnp.concatenate([held[slot, kind, part, at, :, :deep] for slot, at in blocks], axis=0)

    left = [[rows(kind, part) for part in range(2)] for kind in range(2)]
    right = [right_ref[kind, :deep] for kind in range(4)]
    return dot(
        jnp.concatenate([left[0][0], left[0][1], left[0][0], left[0][1], left[1][0], left[1][1]], axis=1),
        jnp.concatenate([right[0], right[1], right[2], right[3], right[0], right[1]], axis=0),
    )


def hop_from(own, index):
    return lax.rem(index - own + RING, RING)


def product_by_hop(place, high_hbm, low_hbm, held, sems, right_ref, hops, store, meanwhile=None):
    owned = high_hbm.shape[3]
    own_core, own_y, own_z = place[2], place[3], place[4]

    def copies(slot, band, strips, at):
        deep = (band + 1) * 2 * owned
        return [
            pltpu.make_async_copy(
                hbm.at[:, band, strips, :, pl.ds(0, deep)],
                held.at[slot, kind, :, at, :, pl.ds(0, deep)],
                sems.at[(slot * RING + band) * 2 + kind],
            )
            for kind, hbm in enumerate((high_hbm, low_hbm))
        ]

    def by_y(band, act):
        hop_y = hop_from(own_y, band)
        for slot, hop in enumerate(hops):

            @pl.when((own_core == 0) & (hop_y == hop))
            def _(slot=slot, hop=hop):
                act(slot, hop, copies(slot, band, slice(None), slice(None)))

    def by_z(band):
        return [
            copy
            for slot, hop in enumerate(hops)
            for copy in copies(slot, band, pl.ds(lax.rem(own_z + hop, RING), 1), pl.ds(band, 1))
        ]

    for band in range(RING):
        by_y(band, lambda slot, hop, moves: [copy.start() for copy in moves])

        @pl.when(own_core == 1)
        def _(band=band):
            for copy in by_z(band):
                copy.start()

    if meanwhile is not None:
        meanwhile()
    for band in range(RING):

        def finish(slot, hop, moves, band=band):
            for copy in moves:
                copy.wait()
            result = band_product(held, right_ref, band, [(slot, strip) for strip in range(RING)])
            for strip in range(RING):
                store(hop, hop_from(own_z, strip), result[strip * owned : (strip + 1) * owned])

        by_y(band, finish)

        @pl.when(own_core == 1)
        def _(band=band):
            for copy in by_z(band):
                copy.wait()
            result = band_product(held, right_ref, band, [(slot, band) for slot in range(len(hops))])
            for at, hop in enumerate(hops):
                store(hop, hop_from(own_y, band), result[at * owned : (at + 1) * owned])


def far_kernel(
    place, high_hbm, low_hbm, own_ref, other_ref, left_ref, right_ref, far_ref, left2_ref, right2_ref, far2_ref,
    right_side, to_left, to_right, held, sems,
):
    owned = own_ref.shape[0]
    own_x, own_core = place[1], place[2]

    def fill():
        for hop, ref, ref2 in (
            (0, own_ref, other_ref), (1, left_ref, left2_ref), (3, right_ref, right2_ref), (2, far_ref, far2_ref)
        ):
            for core, piece in ((own_core, ref), (1 - own_core, ref2)):
                at = pl.multiple_of((hop_from(hop, own_x) * 2 + core) * owned, owned)
                high, low = halves(piece[...])
                for kind, value in enumerate((high, turned(high, SOURCES), low, turned(low, SOURCES))):
                    right_side[kind, pl.ds(at, owned), :] = value

    def store(hop, other_hop, value):
        for at, ref in enumerate((to_left, to_right)):

            @pl.when(other_hop // 2 == at)
            def _(ref=ref):
                ref[lax.rem(other_hop, 2)] = value

    product_by_hop(place, high_hbm, low_hbm, held, sems, right_side, (2,), store, fill)


def near_kernel(place, high_hbm, low_hbm, right_side, left, right, held, sems):
    def store(hop, other_hop, value):
        (left if hop == 1 else right)[other_hop] = value

    product_by_hop(place, high_hbm, low_hbm, held, sems, right_side, (1, 3), store)


def own_kernel(place, high_hbm, low_hbm, right_side, own, held, sems):
    def store(hop, other_hop, value):
        own[other_hop] = value

    product_by_hop(place, high_hbm, low_hbm, held, sems, right_side, (0,), store)


def join_kernel(left, right, got_left, got_right, left_out, right_out):
    left_out[:2] = left[:2] + got_left[...]
    left_out[2:] = left[2:]
    right_out[:2] = right[:2]
    right_out[2:] = right[2:] + got_right[...]


def material_gradient(eliminated, kernel_coef, p_speed, s_speed, density):
    norming = 1.0 / jnp.sqrt(jnp.float32(SOURCES))
    fwd_real, fwd_imag, adj_real, adj_imag = (eliminated[:, at * SOURCES : (at + 1) * SOURCES] for at in range(4))
    k_lambda = jnp.sum(fwd_real * adj_real - fwd_imag * adj_imag, axis=1) * norming
    k_mu = jnp.sum(fwd_real * adj_imag + fwd_imag * adj_real, axis=1) * norming
    k_rho = jnp.sum(fwd_real * adj_real + fwd_imag * adj_imag, axis=1) * norming
    grad_lambda = kernel_coef[0] * k_lambda
    grad_mu = kernel_coef[1] * k_mu
    grad_rho = kernel_coef[2] * k_rho
    first_out = 2.0 * density * p_speed * grad_lambda
    second_out = 2.0 * density * s_speed * (grad_mu - 2.0 * grad_lambda)
    third_out = (
        (p_speed * p_speed - 2.0 * s_speed * s_speed) * grad_lambda
        + s_speed * s_speed * grad_mu
        + grad_rho
    )
    return jnp.stack([first_out, second_out, third_out])


def along(axis, hop):
    if axis == "core":
        return [(i, i ^ 1) for i in range(2 * RING)]
    if axis == "x":
        return [(i, (i + 2 * hop) % (2 * RING)) for i in range(2 * RING)]
    if axis == "y":
        return [(i, (i + RING * hop) % (RING * RING)) for i in range(RING * RING)]
    return [(i, i // RING * RING + (i + hop) % RING) for i in range(RING * RING)]


def move(value, axis, hop=1):
    return lax.ppermute(value, "row" if axis in ("x", "core") else "col", along(axis, hop))


def move_by_core(value, phase, hop):
    pairs = []
    for row in range(2 * RING):
        axis = "yz"[(row + phase) % 2]
        pairs += [(row * RING * RING + former, row * RING * RING + latter) for former, latter in along(axis, hop)]
    return lax.ppermute(value, ("row", "col"), pairs)


def params(mebibytes, **more):
    return pltpu.CompilerParams(vmem_limit_bytes=mebibytes << 20, **more)


SMEM = pl.BlockSpec(memory_space=pltpu.SMEM)
VMEM = pl.BlockSpec(memory_space=pltpu.VMEM)
ANY = pl.BlockSpec(memory_space=pl.ANY)


def per_device(
    leaf_source,
    leaf_inv,
    leaf_low,
    child_count,
    child_owner,
    child_slot,
    parent_source,
    parent_inv,
    kernel_coef,
    p_speed,
    s_speed,
    density,
):
    row, col = lax.axis_index("row"), lax.axis_index("col")
    devices = lax.axis_size("row") * lax.axis_size("col")
    owned = parent_source.shape[1]
    width = 2 * parent_source.shape[2]
    place = jnp.stack([row * lax.axis_size("col") + col, row // 2, row % 2, col // RING, col % RING])
    contrib = child_slot.shape[1]
    position = jnp.arange(contrib, dtype=jnp.int32)
    owner = jnp.where(position[None, :] < child_count[:, None], child_owner[:, :, 0], -1)

    outgoing = pl.pallas_call(
        leaf_kernel,
        out_shape=jax.ShapeDtypeStruct((devices * CAPACITY * width // LANES, LANES), F32),
        in_specs=[SMEM, SMEM] + [ANY] * 4,
        out_specs=VMEM,
        scratch_shapes=[
            pltpu.VMEM((1, contrib), jnp.int32),
            pltpu.VMEM((2,) + leaf_source.shape[2:], F32),
            pltpu.VMEM(leaf_inv.shape[1:], F32),
            pltpu.VMEM(leaf_low.shape[1:], F32),
            pltpu.SemaphoreType.DMA((4,)),
        ],
        compiler_params=params(60),
        name="leaf",
    )(place, child_count, child_owner.reshape(devices, 1, contrib), leaf_source[:, 0], leaf_inv[0], leaf_low[0])
    rows, depth = parent_inv.shape[1:]
    block = rows // 8
    block_spec = pl.BlockSpec((2, block, depth), lambda i: (0, i, 0))
    inv_high, inv_low, token = pl.pallas_call(
        split_kernel,
        out_shape=[jax.ShapeDtypeStruct(parent_inv.shape, BF16)] * 2 + [jax.ShapeDtypeStruct((8, LANES), F32)],
        grid=(rows // block,),
        in_specs=[block_spec, ANY],
        out_specs=[block_spec] * 2 + [pl.BlockSpec((8, LANES), lambda i: (0, 0))],
        compiler_params=params(60),
        cost_estimate=pl.CostEstimate(flops=4 * rows * depth, bytes_accessed=16 * rows * depth, transcendentals=0),
        name="split",
    )(parent_inv, outgoing)
    banded = (2, RING, RING, owned, depth)
    inv_high, inv_low = inv_high.reshape(banded), inv_low.reshape(banded)
    placing = pl.pallas_call(
        placing_kernel,
        out_shape=jax.ShapeDtypeStruct((CAPACITY, devices, owned), BF16),
        in_specs=[SMEM] + [VMEM] * 2 + [ANY],
        out_specs=VMEM,
        compiler_params=params(16),
        cost_estimate=pl.CostEstimate(flops=2 * devices * 512 * 512, bytes_accessed=1 << 20, transcendentals=0),
        name="placing",
    )(place, owner, child_slot, token)
    arrived = lax.all_to_all(
        outgoing.reshape(devices, -1, LANES), ("row", "col"), split_axis=0, concat_axis=0, tiled=True
    )
    assembled = pl.pallas_call(
        extend_kernel,
        out_shape=jax.ShapeDtypeStruct((owned, width), F32),
        in_specs=[VMEM] * 3,
        out_specs=VMEM,
        compiler_params=params(16),
        name="extend",
    )(placing, arrived.reshape(outgoing.shape), parent_source)

    other = move(assembled, "core")
    hops = [move(assembled, "x", hop) for hop in (1, 3, 2)]
    swapped = [move(value, "core") for value in hops]

    two = jax.ShapeDtypeStruct((2, owned, width), F32)
    four = jax.ShapeDtypeStruct((RING, owned, width), F32)

    def held_scratch(count):
        return [
            pltpu.VMEM((count, 2, 2, RING, owned, depth), BF16),
            pltpu.SemaphoreType.DMA((count * RING * 2,)),
        ]

    right_side, to_left, to_right = pl.pallas_call(
        far_kernel,
        out_shape=[jax.ShapeDtypeStruct((4, depth, width), BF16), two, two],
        in_specs=[SMEM, ANY, ANY] + [VMEM] * 8,
        out_specs=[VMEM] * 3,
        scratch_shapes=held_scratch(1),
        compiler_params=params(46),
        name="far",
    )(place, inv_high, inv_low, assembled, other, *hops, *swapped)

    def product(kernel, name, count):
        return pl.pallas_call(
            kernel,
            out_shape=[four] * count,
            in_specs=[SMEM, ANY, ANY, VMEM],
            out_specs=[VMEM] * count,
            scratch_shapes=held_scratch(count),
            compiler_params=params(44),
            cost_estimate=pl.CostEstimate(
                flops=count * 6 * rows * depth * width, bytes_accessed=1 << 20, transcendentals=0
            ),
            name=name,
        )(place, inv_high, inv_low, right_side)

    got_left, got_right = move_by_core(to_left, 0, 1), move_by_core(to_right, 0, 3)
    left, right = product(near_kernel, "near", 2)
    left, right = pl.pallas_call(
        join_kernel,
        out_shape=[four] * 2,
        in_specs=[VMEM] * 4,
        out_specs=[VMEM] * 2,
        compiler_params=params(16),
        name="join",
    )(left, right, got_left, got_right)
    got_left, got_right = move_by_core(left, 0, 1), move_by_core(right, 0, 3)
    (own,) = product(own_kernel, "own", 1)
    plane = own + got_left + got_right
    then = [move_by_core(plane[hop], 1, hop) for hop in (1, 3, 2)]
    eliminated = plane[0] + then[0] + then[1] + then[2]
    return material_gradient(eliminated, kernel_coef, p_speed, s_speed, density)


def solution(mesh):
    return jax.shard_map(
        per_device,
        mesh=mesh,
        in_specs=(
            P(None, ("row", "col"), None, None),
            P(("row", "col"), None, None, None),
            P(("row", "col"), None, None, None),
            P(),
            P(),
            P(),
            P(None, ("row", "col"), None),
            P(None, "row", "col"),
            P(None, ("row", "col")),
            P(("row", "col")),
            P(("row", "col")),
            P(("row", "col")),
        ),
        out_specs=P(None, ("row", "col")),
        check_vma=False,
    )
```

```python
import functools

import jax
import jax.numpy as jnp
from jax import lax
from jax.experimental import pallas as pl
from jax.experimental.pallas import tpu as pltpu
from jax.sharding import PartitionSpec as P

SOURCES = 128
CAPACITY = 6
LANES = 128
RING = 4
BATCHES = ((2, 0), (1, 3))
F32 = jnp.float32
BF16 = jnp.bfloat16


def halves(value):
    high = value.astype(BF16)
    return high, (value - high.astype(F32)).astype(BF16)


def dot(left, right, dims=((1,), (0,))):
    return lax.dot_general(left, right, (dims, ((), ())), preferred_element_type=F32)


def left_parts(real_part, imag_part):
    real_high, real_low = halves(real_part)
    imag_high, imag_low = halves(imag_part)
    return jnp.concatenate([real_high, imag_high, real_high, imag_high, real_low, imag_low], axis=1)


def turned(value, part_width):
    parts = [value[:, at : at + part_width] for at in range(0, value.shape[1], part_width)]
    return jnp.concatenate(
        [part for at in range(0, len(parts), 2) for part in (-parts[at + 1], parts[at])], axis=1
    )


def right_parts(value):
    high, low = halves(value)
    turned_high, turned_low = (turned(part, value.shape[1] // 2) for part in (high, low))
    return jnp.concatenate([high, turned_high, low, turned_low, high, turned_high], axis=0)


def whereabouts():
    row, col = lax.axis_index("row"), lax.axis_index("col")
    return row * lax.axis_size("col") + col, row // 2, lax.rem(row, 2), col // RING, lax.rem(col, RING)


def running_count(mask):
    length = mask.shape[1]
    former = lax.broadcasted_iota(jnp.int32, (length, length), 0)
    latter = lax.broadcasted_iota(jnp.int32, (length, length), 1)
    upto = jnp.where(former <= latter, 1.0, 0.0).astype(BF16)
    return dot(mask.astype(BF16), upto)


def leaf_kernel(
    count_ref, owner_hbm, source_hbm, inv_hbm, low_hbm, out_ref, owner_ref, source_ref, inv_ref, low_ref, sems
):
    devices, contrib = owner_hbm.shape[0], owner_ref.shape[1]
    myself = whereabouts()[0]
    pivots, breadth = inv_ref.shape[1], source_ref.shape[2]
    groups = 2 * breadth // LANES
    copies = [
        pltpu.make_async_copy(former, latter, sems.at[i])
        for i, (former, latter) in enumerate(
            (
                (source_hbm, source_ref),
                (inv_hbm, inv_ref),
                (owner_hbm.at[myself], owner_ref),
                (low_hbm, low_ref),
            )
        )
    ]
    for copy in copies:
        copy.start()
    copies[2].wait()
    names = lax.broadcasted_iota(jnp.int32, (devices, contrib), 0)
    position = lax.broadcasted_iota(jnp.int32, (devices, contrib), 1)
    chosen = jnp.where((names == owner_ref[...]) & (position < count_ref[myself]), 1.0, 0.0)
    rank = running_count(chosen) * chosen
    pick = jnp.concatenate(
        [jnp.where(rank == k + 1.0, 1.0, 0.0).astype(BF16) for k in range(CAPACITY)], axis=0
    )
    copies[0].wait()
    pivot_source = jnp.concatenate([source_ref[0, :pivots], source_ref[1, :pivots]], axis=1)
    copies[1].wait()
    half = pivots // 2
    upper = dot(
        left_parts(inv_ref[0, :half, :half], inv_ref[1, :half, :half]), right_parts(pivot_source[:half])
    )
    lower = dot(left_parts(inv_ref[0, half:], inv_ref[1, half:]), right_parts(pivot_source))
    pivot_part = jnp.concatenate([upper, lower], axis=0)
    copies[3].wait()
    eliminated = dot(left_parts(low_ref[0], low_ref[1]), right_parts(pivot_part))
    update = jnp.concatenate([source_ref[0, pivots:], source_ref[1, pivots:]], axis=1) - eliminated
    high, low = halves(update)
    rows = dot(jnp.concatenate([pick, pick], axis=1), jnp.concatenate([high, low], axis=0))
    for k in range(CAPACITY):
        for g in range(groups):
            at = (g % 2) * breadth + g // 2 * LANES
            out_ref[pl.ds(k * groups + g, devices, stride=CAPACITY * groups), :] = rows[
                k * devices : (k + 1) * devices, at : at + LANES
            ]


def placing_kernel(owner_ref, slot_ref, token_hbm, out_ref):
    del token_hbm
    devices = owner_ref.shape[0]
    owned = out_ref.shape[2]
    mine = jnp.where(owner_ref[...] == whereabouts()[0], 1.0, 0.0)
    rank = running_count(mine) * mine
    slots = slot_ref[...].astype(F32) + 1.0
    rows = lax.broadcasted_iota(jnp.int32, (devices, owned), 1).astype(F32) + 1.0
    for k in range(CAPACITY):
        slot = jnp.sum(jnp.where(rank == k + 1.0, slots, 0.0), axis=1, keepdims=True)
        out_ref[k] = jnp.where(slot == rows, 1.0, 0.0).astype(BF16)


def extend_kernel(placing_ref, arrived_ref, parent_ref, out_ref):
    devices = placing_ref.shape[1]
    groups = out_ref.shape[1] // LANES
    for g in range(groups):
        total = parent_ref[g % 2, :, g // 2 * LANES : (g // 2 + 1) * LANES]
        for k in range(CAPACITY):
            rows = arrived_ref[pl.ds(k * groups + g, devices, stride=CAPACITY * groups), :]
            high, low = halves(rows)
            total += dot(placing_ref[k], high, ((0,), (0,)))
            total += dot(placing_ref[k], low, ((0,), (0,)))
        out_ref[:, g * LANES : (g + 1) * LANES] = total


def first_unit(band, strip=0):
    return 2 * band * (band + 1) + strip * (band + 1)


UNITS = first_unit(RING)


def split_kernel(value_ref, after_hbm, out_ref, token_ref):
    del after_hbm
    token_ref[...] = jnp.zeros_like(token_ref)
    step = pl.program_id(0)
    rows, columns = out_ref.shape[3:]
    strips = value_ref.shape[1] // rows
    steps = RING // strips
    for band in range(RING):

        @pl.when(step // steps == band)
        def _(band=band):
            for j in range(strips):
                strip = lax.rem(step, steps) * strips + j
                for piece in range(band + 1):
                    for part in range(2):
                        value = value_ref[part, j * rows : (j + 1) * rows, piece * columns : (piece + 1) * columns]
                        high, low = halves(value)
                        out_ref[first_unit(band, strip) + piece, 0, part] = high
                        out_ref[first_unit(band, strip) + piece, 1, part] = low


def band_product(held, right_ref, band, strips):
    deep = (band + 1) * held.shape[4]

    def rows(kind, part):
        return jnp.concatenate(
            [
                jnp.concatenate([held[first_unit(band, strip) + piece, kind, part] for piece in range(band + 1)], axis=1)
                for strip in strips
            ],
            axis=0,
        )

    left = [[rows(kind, part) for part in range(2)] for kind in range(2)]
    right = [right_ref[kind, :deep] for kind in range(4)]
    return dot(
        jnp.concatenate([left[0][0], left[0][1], left[0][0], left[0][1], left[1][0], left[1][1]], axis=1),
        jnp.concatenate([right[0], right[1], right[2], right[3], right[0], right[1]], axis=0),
    )


def hop_from(own, index):
    return lax.rem(index - own + RING, RING)


def each_copy(units_hbm, held, sems, hops, act):
    _, _, own_core, own_y, own_z = whereabouts()

    def copy(first, count, sem):
        act(pltpu.make_async_copy(units_hbm.at[pl.ds(first, count)], held.at[pl.ds(first, count)], sems.at[sem]))

    for hop in hops:
        for band in range(RING):

            @pl.when((own_core == 0) & (hop_from(own_y, band) == hop))
            def _(band=band):
                copy(first_unit(band), RING * (band + 1), band)

        @pl.when(own_core == 1)
        def _(hop=hop):
            for band in range(RING):
                copy(first_unit(band, lax.rem(own_z + hop, RING)), band + 1, hop * RING + band)


def start_rows(*args):
    each_copy(*args, lambda copy: copy.start())


def wait_rows(*args):
    each_copy(*args, lambda copy: copy.wait())


def product_by_hop(held, right_ref, hops, store):
    owned = held.shape[3]
    _, _, own_core, own_y, own_z = whereabouts()
    for band in range(RING):
        for hop in hops:

            @pl.when((own_core == 0) & (hop_from(own_y, band) == hop))
            def _(band=band, hop=hop):
                result = band_product(held, right_ref, band, range(RING))
                for strip in range(RING):
                    store(hop, hop_from(own_z, strip), result[strip * owned : (strip + 1) * owned])

        @pl.when(own_core == 1)
        def _(band=band):
            result = band_product(held, right_ref, band, [lax.rem(own_z + hop, RING) for hop in hops])
            for at, hop in enumerate(hops):
                store(hop, hop_from(own_y, band), result[at * owned : (at + 1) * owned])


def far_kernel(
    units_hbm, own_ref, other_ref, left_ref, right_ref, far_ref, left2_ref, right2_ref, far2_ref,
    right_side, to_left, to_right, held, sems,
):
    owned = own_ref.shape[0]
    _, own_x, own_core, _, _ = whereabouts()

    def fill():
        for hop, ref, ref2 in (
            (0, own_ref, other_ref), (1, left_ref, left2_ref), (3, right_ref, right2_ref), (2, far_ref, far2_ref)
        ):
            for core, piece in ((own_core, ref), (1 - own_core, ref2)):
                at = pl.multiple_of((hop_from(hop, own_x) * 2 + core) * owned, owned)
                high, low = halves(piece[...])
                for kind, value in enumerate((high, turned(high, SOURCES), low, turned(low, SOURCES))):
                    right_side[kind, pl.ds(at, owned), :] = value

    def store(hop, other_hop, value):
        for at, ref in enumerate((to_left, to_right)):

            @pl.when(other_hop // 2 == at)
            def _(ref=ref):
                ref[lax.rem(other_hop, 2)] = value

    start_rows(units_hbm, held, sems, (2,))
    start_rows(units_hbm, held, sems, (1, 3, 0))
    fill()
    wait_rows(units_hbm, held, sems, (2,))
    product_by_hop(held, right_side, (2,), store)
    wait_rows(units_hbm, held, sems, (1, 3, 0))


def near_kernel(held, right_side, left, right):
    def store(hop, other_hop, value):
        (left if hop == 1 else right)[other_hop] = value

    product_by_hop(held, right_side, (1, 3), store)


def own_kernel(held, right_side, own):
    def store(hop, other_hop, value):
        own[other_hop] = value

    product_by_hop(held, right_side, (0,), store)


def join_kernel(left, right, got_left, got_right, *outs):
    for hops, (left_out, right_out) in zip(BATCHES, (outs[:2], outs[2:])):
        for at, hop in enumerate(hops):
            left_out[at] = left[hop] + got_left[hop] if hop < 2 else left[hop]
            right_out[at] = right[hop] + got_right[hop - 2] if hop >= 2 else right[hop]


def settle_kernel(hops, own, got_left, got_right, *outs):
    for at, (hop, out) in enumerate(zip(hops, outs)):
        out[...] = own[hop] + got_left[at] + got_right[at]


def material_gradient(eliminated, kernel_coef, p_speed, s_speed, density):
    norming = 1.0 / jnp.sqrt(jnp.float32(SOURCES))
    fwd_real, fwd_imag, adj_real, adj_imag = (eliminated[:, at * SOURCES : (at + 1) * SOURCES] for at in range(4))
    k_lambda = jnp.sum(fwd_real * adj_real - fwd_imag * adj_imag, axis=1) * norming
    k_mu = jnp.sum(fwd_real * adj_imag + fwd_imag * adj_real, axis=1) * norming
    k_rho = jnp.sum(fwd_real * adj_real + fwd_imag * adj_imag, axis=1) * norming
    grad_lambda = kernel_coef[0] * k_lambda
    grad_mu = kernel_coef[1] * k_mu
    grad_rho = kernel_coef[2] * k_rho
    first_out = 2.0 * density * p_speed * grad_lambda
    second_out = 2.0 * density * s_speed * (grad_mu - 2.0 * grad_lambda)
    third_out = (
        (p_speed * p_speed - 2.0 * s_speed * s_speed) * grad_lambda
        + s_speed * s_speed * grad_mu
        + grad_rho
    )
    return jnp.stack([first_out, second_out, third_out])


def along(axis, hop):
    if axis == "core":
        return [(i, i ^ 1) for i in range(2 * RING)]
    if axis == "x":
        return [(i, (i + 2 * hop) % (2 * RING)) for i in range(2 * RING)]
    if axis == "y":
        return [(i, (i + RING * hop) % (RING * RING)) for i in range(RING * RING)]
    return [(i, i // RING * RING + (i + hop) % RING) for i in range(RING * RING)]


def move(value, axis, hop=1):
    return lax.ppermute(value, "row" if axis in ("x", "core") else "col", along(axis, hop))


def move_by_core(value, phase, hop):
    pairs = []
    for row in range(2 * RING):
        axis = "yz"[(row + phase) % 2]
        pairs += [(row * RING * RING + former, row * RING * RING + latter) for former, latter in along(axis, hop)]
    return lax.ppermute(value, ("row", "col"), pairs)


def params(mebibytes, **more):
    return pltpu.CompilerParams(vmem_limit_bytes=mebibytes << 20, **more)


SMEM = pl.BlockSpec(memory_space=pltpu.SMEM)
VMEM = pl.BlockSpec(memory_space=pltpu.VMEM)
ANY = pl.BlockSpec(memory_space=pl.ANY)


def per_device(
    leaf_source,
    leaf_inv,
    leaf_low,
    child_count,
    child_owner,
    child_slot,
    parent_source,
    parent_inv,
    kernel_coef,
    p_speed,
    s_speed,
    density,
):
    devices = lax.axis_size("row") * lax.axis_size("col")
    owned = parent_source.shape[1]
    width = 2 * parent_source.shape[2]
    contrib = child_slot.shape[1]
    position = jnp.arange(contrib, dtype=jnp.int32)
    owner = jnp.where(position[None, :] < child_count[:, None], child_owner[:, :, 0], -1)

    outgoing = pl.pallas_call(
        leaf_kernel,
        out_shape=jax.ShapeDtypeStruct((devices * CAPACITY * width // LANES, LANES), F32),
        in_specs=[SMEM] + [ANY] * 4,
        out_specs=VMEM,
        scratch_shapes=[
            pltpu.VMEM((1, contrib), jnp.int32),
            pltpu.VMEM((2,) + leaf_source.shape[2:], F32),
            pltpu.VMEM(leaf_inv.shape[1:], F32),
            pltpu.VMEM(leaf_low.shape[1:], F32),
            pltpu.SemaphoreType.DMA((4,)),
        ],
        compiler_params=params(60),
        name="leaf",
    )(child_count, child_owner.reshape(devices, 1, contrib), leaf_source[:, 0], leaf_inv[0], leaf_low[0])
    rows, depth = parent_inv.shape[1:]
    block = rows // 8
    block_spec = pl.BlockSpec((2, block, depth), lambda i: (0, i, 0))
    units_shape = jax.ShapeDtypeStruct((UNITS, 2, 2, owned, depth // RING), BF16)
    units, token = pl.pallas_call(
        split_kernel,
        out_shape=[units_shape, jax.ShapeDtypeStruct((8, LANES), F32)],
        grid=(rows // block,),
        in_specs=[block_spec, ANY],
        out_specs=[pl.BlockSpec(units_shape.shape, lambda i: (0,) * 5), pl.BlockSpec((8, LANES), lambda i: (0, 0))],
        compiler_params=params(60),
        cost_estimate=pl.CostEstimate(flops=4 * rows * depth, bytes_accessed=16 * rows * depth, transcendentals=0),
        name="split",
    )(parent_inv, outgoing)
    placing = pl.pallas_call(
        placing_kernel,
        out_shape=jax.ShapeDtypeStruct((CAPACITY, devices, owned), BF16),
        in_specs=[VMEM] * 2 + [ANY],
        out_specs=VMEM,
        compiler_params=params(16),
        cost_estimate=pl.CostEstimate(flops=2 * devices * 512 * 512, bytes_accessed=1 << 20, transcendentals=0),
        name="placing",
    )(owner, child_slot, token)
    arrived = lax.all_to_all(
        outgoing.reshape(devices, -1, LANES), ("row", "col"), split_axis=0, concat_axis=0, tiled=True
    )
    assembled = pl.pallas_call(
        extend_kernel,
        out_shape=jax.ShapeDtypeStruct((owned, width), F32),
        in_specs=[VMEM] * 3,
        out_specs=VMEM,
        compiler_params=params(16),
        name="extend",
    )(placing, arrived.reshape(outgoing.shape), parent_source)

    other = move(assembled, "core")
    hops = [move(assembled, "x", hop) for hop in (1, 3, 2)]
    swapped = [move(value, "core") for value in hops]

    two = jax.ShapeDtypeStruct((2, owned, width), F32)
    four = jax.ShapeDtypeStruct((RING, owned, width), F32)

    def cost(blocks):
        return pl.CostEstimate(flops=blocks * 6 * rows * depth * width, bytes_accessed=1 << 20, transcendentals=0)

    right_side, to_left, to_right, held = pl.pallas_call(
        far_kernel,
        out_shape=[jax.ShapeDtypeStruct((4, depth, width), BF16), two, two, units_shape],
        in_specs=[ANY] + [VMEM] * 8,
        out_specs=[VMEM] * 4,
        scratch_shapes=[pltpu.SemaphoreType.DMA((RING * RING,))],
        compiler_params=params(33),
        name="far",
    )(units, assembled, other, *hops, *swapped)
    got_left, got_right = move_by_core(to_left, 0, 1), move_by_core(to_right, 0, 3)
    left, right = pl.pallas_call(
        near_kernel,
        out_shape=[four] * 2,
        in_specs=[VMEM] * 2,
        out_specs=[VMEM] * 2,
        compiler_params=params(36),
        cost_estimate=cost(2),
        name="near",
    )(held, right_side)
    joined = pl.pallas_call(
        join_kernel,
        out_shape=[two] * 4,
        in_specs=[VMEM] * 4,
        out_specs=[VMEM] * 4,
        compiler_params=params(16),
        name="join",
    )(left, right, got_left, got_right)
    got = [move_by_core(value, 0, (1, 3)[at % 2]) for at, value in enumerate(joined)]
    own = pl.pallas_call(
        own_kernel,
        out_shape=four,
        in_specs=[VMEM] * 2,
        out_specs=VMEM,
        compiler_params=params(36),
        cost_estimate=cost(1),
        name="own",
    )(held, right_side)
    parts = []
    for at, hops in enumerate(BATCHES):
        values = pl.pallas_call(
            functools.partial(settle_kernel, hops),
            out_shape=[jax.ShapeDtypeStruct((owned, width), F32)] * 2,
            in_specs=[VMEM] * 3,
            out_specs=[VMEM] * 2,
            compiler_params=params(16),
            name="settle",
        )(own, got[2 * at], got[2 * at + 1])
        parts += [move_by_core(value, 1, hop) if hop else value for value, hop in zip(values, hops)]
    eliminated = functools.reduce(jnp.add, parts)
    return material_gradient(eliminated, kernel_coef, p_speed, s_speed, density)


def solution(mesh):
    return jax.shard_map(
        per_device,
        mesh=mesh,
        in_specs=(
            P(None, ("row", "col"), None, None),
            P(("row", "col"), None, None, None),
            P(("row", "col"), None, None, None),
            P(),
            P(),
            P(),
            P(None, ("row", "col"), None),
            P(None, "row", "col"),
            P(None, ("row", "col")),
            P(("row", "col")),
            P(("row", "col")),
            P(("row", "col")),
        ),
        out_specs=P(None, ("row", "col")),
        check_vma=False,
    )
```

```python
import functools

import jax
import jax.numpy as jnp
from jax import lax
from jax.experimental import pallas as pl
from jax.experimental.pallas import tpu as pltpu
from jax.sharding import PartitionSpec as P

SOURCES = 128
CAPACITY = 6
LANES = 128
RING = 4
F32 = jnp.float32
BF16 = jnp.bfloat16


def halves(value):
    high = value.astype(BF16)
    return high, (value - high.astype(F32)).astype(BF16)


def dot(left, right, dims=((1,), (0,))):
    return lax.dot_general(left, right, (dims, ((), ())), preferred_element_type=F32)


def left_parts(real_part, imag_part):
    real_high, real_low = halves(real_part)
    imag_high, imag_low = halves(imag_part)
    return jnp.concatenate([real_high, imag_high, real_high, imag_high, real_low, imag_low], axis=1)


def turned(value, part_width):
    parts = [value[:, at : at + part_width] for at in range(0, value.shape[1], part_width)]
    return jnp.concatenate(
        [part for at in range(0, len(parts), 2) for part in (-parts[at + 1], parts[at])], axis=1
    )


def right_parts(value):
    high, low = halves(value)
    turned_high, turned_low = (turned(part, value.shape[1] // 2) for part in (high, low))
    return jnp.concatenate([high, turned_high, low, turned_low, high, turned_high], axis=0)


def whereabouts():
    row, col = lax.axis_index("row"), lax.axis_index("col")
    return row * lax.axis_size("col") + col, row // 2, lax.rem(row, 2), col // RING, lax.rem(col, RING)


def running_count(mask):
    length = mask.shape[1]
    former = lax.broadcasted_iota(jnp.int32, (length, length), 0)
    latter = lax.broadcasted_iota(jnp.int32, (length, length), 1)
    upto = jnp.where(former <= latter, 1.0, 0.0).astype(BF16)
    return dot(mask.astype(BF16), upto)


def leaf_kernel(
    count_ref, owner_hbm, source_hbm, inv_hbm, low_hbm, out_ref, owner_ref, source_ref, inv_ref, low_ref, sems
):
    devices, contrib = owner_hbm.shape[0], owner_ref.shape[1]
    myself = whereabouts()[0]
    pivots, breadth = inv_ref.shape[1], source_ref.shape[2]
    groups = 2 * breadth // LANES
    copies = [
        pltpu.make_async_copy(former, latter, sems.at[i])
        for i, (former, latter) in enumerate(
            (
                (source_hbm.at[:, pl.ds(0, pivots)], source_ref.at[:, pl.ds(0, pivots)]),
                (inv_hbm, inv_ref),
                (owner_hbm.at[myself], owner_ref),
                (low_hbm, low_ref),
                (source_hbm.at[:, pl.ds(pivots, contrib)], source_ref.at[:, pl.ds(pivots, contrib)]),
            )
        )
    ]
    for at in (2, 0, 1, 3, 4):
        copies[at].start()
    copies[2].wait()
    names = lax.broadcasted_iota(jnp.int32, (devices, contrib), 0)
    position = lax.broadcasted_iota(jnp.int32, (devices, contrib), 1)
    chosen = jnp.where((names == owner_ref[...]) & (position < count_ref[myself]), 1.0, 0.0)
    rank = running_count(chosen) * chosen
    pick = jnp.concatenate(
        [jnp.where(rank == k + 1.0, 1.0, 0.0).astype(BF16) for k in range(CAPACITY)], axis=0
    )
    copies[0].wait()
    pivot_source = jnp.concatenate([source_ref[0, :pivots], source_ref[1, :pivots]], axis=1)
    copies[1].wait()
    half = pivots // 2
    upper = dot(
        left_parts(inv_ref[0, :half, :half], inv_ref[1, :half, :half]), right_parts(pivot_source[:half])
    )
    lower = dot(left_parts(inv_ref[0, half:], inv_ref[1, half:]), right_parts(pivot_source))
    pivot_part = jnp.concatenate([upper, lower], axis=0)
    copies[3].wait()
    eliminated = dot(left_parts(low_ref[0], low_ref[1]), right_parts(pivot_part))
    copies[4].wait()
    update = jnp.concatenate([source_ref[0, pivots:], source_ref[1, pivots:]], axis=1) - eliminated
    high, low = halves(update)
    rows = dot(jnp.concatenate([pick, pick], axis=1), jnp.concatenate([high, low], axis=0))
    for k in range(CAPACITY):
        for g in range(groups):
            at = (g % 2) * breadth + g // 2 * LANES
            out_ref[pl.ds(k * groups + g, devices, stride=CAPACITY * groups), :] = rows[
                k * devices : (k + 1) * devices, at : at + LANES
            ]


def placing_kernel(owner_ref, slot_ref, token_hbm, out_ref):
    del token_hbm
    devices = owner_ref.shape[0]
    owned = out_ref.shape[2]
    mine = jnp.where(owner_ref[...] == whereabouts()[0], 1.0, 0.0)
    rank = running_count(mine) * mine
    slots = slot_ref[...].astype(F32) + 1.0
    rows = lax.broadcasted_iota(jnp.int32, (devices, owned), 1).astype(F32) + 1.0
    for k in range(CAPACITY):
        slot = jnp.sum(jnp.where(rank == k + 1.0, slots, 0.0), axis=1, keepdims=True)
        out_ref[k] = jnp.where(slot == rows, 1.0, 0.0).astype(BF16)


def extend_kernel(placing_ref, arrived_ref, parent_ref, out_ref):
    devices = placing_ref.shape[1]
    groups = out_ref.shape[1] // LANES
    for g in range(groups):
        total = parent_ref[g % 2, :, g // 2 * LANES : (g // 2 + 1) * LANES]
        for k in range(CAPACITY):
            rows = arrived_ref[pl.ds(k * groups + g, devices, stride=CAPACITY * groups), :]
            high, low = halves(rows)
            total += dot(placing_ref[k], high, ((0,), (0,)))
            total += dot(placing_ref[k], low, ((0,), (0,)))
        out_ref[:, g * LANES : (g + 1) * LANES] = total


def first_unit(band, strip=0):
    return 2 * band * (band + 1) + strip * (band + 1)


UNITS = first_unit(RING)


def split_kernel(value_ref, after_hbm, out_ref, token_ref):
    del after_hbm
    token_ref[...] = jnp.zeros_like(token_ref)
    step = pl.program_id(0)
    rows, columns = out_ref.shape[3:]
    strips = value_ref.shape[1] // rows
    steps = RING // strips
    for band in range(RING):

        @pl.when(step // steps == band)
        def _(band=band):
            for j in range(strips):
                strip = lax.rem(step, steps) * strips + j
                for piece in range(band + 1):
                    for part in range(2):
                        value = value_ref[part, j * rows : (j + 1) * rows, piece * columns : (piece + 1) * columns]
                        high, low = halves(value)
                        out_ref[first_unit(band, strip) + piece, 0, part] = high
                        out_ref[first_unit(band, strip) + piece, 1, part] = low


def piece_product(held, right_ref, units, piece):
    depth = held.shape[4]

    def rows(kind, part):
        return jnp.concatenate([held[unit, kind, part] for unit in units], axis=0)

    high, low = ([rows(kind, part) for part in range(2)] for kind in range(2))
    right = [right_ref[kind, pl.ds(pl.multiple_of(piece * depth, depth), depth)] for kind in range(4)]
    return dot(
        jnp.concatenate([high[0], high[1], high[0], high[1], low[0], low[1]], axis=1),
        jnp.concatenate([right[0], right[1], right[2], right[3], right[0], right[1]], axis=0),
    )


def hop_from(own, index):
    return lax.rem(index - own + RING, RING)


def each_copy(units_hbm, held, sems, hops, act):
    _, _, own_core, own_y, own_z = whereabouts()

    def copy(first, count, sem):
        act(pltpu.make_async_copy(units_hbm.at[pl.ds(first, count)], held.at[pl.ds(first, count)], sems.at[sem]))

    for hop in hops:
        for band in range(RING):

            @pl.when((own_core == 0) & (hop_from(own_y, band) == hop))
            def _(band=band):
                copy(first_unit(band), RING * (band + 1), band)

        @pl.when(own_core == 1)
        def _(hop=hop):
            for band in range(RING):
                copy(first_unit(band, lax.rem(own_z + hop, RING)), band + 1, hop * RING + band)


def start_rows(*args):
    each_copy(*args, lambda copy: copy.start())


def wait_rows(*args):
    each_copy(*args, lambda copy: copy.wait())


def product_by_hop(held, right_ref, total, hop, store):
    owned = held.shape[3]
    _, _, own_core, own_y, own_z = whereabouts()

    @pl.when(own_core == 0)
    def _():
        band = lax.rem(own_y + hop, RING)
        total[...] = jnp.zeros_like(total)

        def add(piece, carry):
            units = [first_unit(band, strip) + piece for strip in range(RING)]
            total[...] += piece_product(held, right_ref, units, piece)
            return carry

        lax.fori_loop(0, band + 1, add, 0)
        for strip in range(RING):
            store(hop, hop_from(own_z, strip), total[strip * owned : (strip + 1) * owned])

    @pl.when(own_core == 1)
    def _():
        strip = lax.rem(own_z + hop, RING)
        for piece in range(RING):
            units = [first_unit(band, strip) + piece for band in range(piece, RING)]
            value = piece_product(held, right_ref, units, piece)
            if piece:
                total[piece * owned :] += value
            else:
                total[...] = value
        for band in range(RING):
            store(hop, hop_from(own_y, band), total[band * owned : (band + 1) * owned])


def first_axis_odd():
    _, _, own_core, own_y, own_z = whereabouts()
    odd_y, odd_z = lax.rem(own_y, 2), lax.rem(own_z, 2)
    return jnp.where(own_core == 0, odd_y, odd_z), jnp.where(own_core == 0, odd_z, odd_y)


def store_turned(refs, which, slot, value):
    for at, ref in enumerate(refs):

        @pl.when(which == at)
        def _(ref=ref):
            ref[slot] = value


def far_kernel(
    units_hbm, own_ref, other_ref, near_ref, next_ref, far_ref, near2_ref, next2_ref, far2_ref,
    right_side, first, second, held, sems, total,
):
    owned = own_ref.shape[0]
    _, own_x, own_core, _, _ = whereabouts()

    def fill():
        odd_x = lax.rem(own_x, 2)
        for hop, ref, ref2 in (
            (0, own_ref, other_ref), (1 + 2 * odd_x, near_ref, near2_ref), (3 - 2 * odd_x, next_ref, next2_ref), (2, far_ref, far2_ref)
        ):
            for core, piece in ((own_core, ref), (1 - own_core, ref2)):
                at = pl.multiple_of((lax.rem(own_x + hop, RING) * 2 + core) * owned, owned)
                high, low = halves(piece[...])
                for kind, value in enumerate((high, turned(high, SOURCES), low, turned(low, SOURCES))):
                    right_side[kind, pl.ds(at, owned), :] = value

    odd, _ = first_axis_odd()

    def store(hop, other_hop, value):
        store_turned((first, second), lax.rem(other_hop // 2 + odd, 2), lax.rem(other_hop, 2), value)

    start_rows(units_hbm, held, sems, (2,))
    start_rows(units_hbm, held, sems, (1, 3, 0))
    fill()
    wait_rows(units_hbm, held, sems, (2,))
    product_by_hop(held, right_side, total, 2, store)
    wait_rows(units_hbm, held, sems, (1, 3, 0))


def near_kernel(way, held, right_side, after_any, free, joined, total):
    del after_any
    odd, _ = first_axis_odd()
    hop = 1 + 2 * lax.rem(way + odd, 2)

    def store(hop, other_hop, value):
        store_turned((free, joined), jnp.where(other_hop // 2 == hop // 2, 1, 0), lax.rem(other_hop, 2), value)

    product_by_hop(held, right_side, total, hop, store)


def own_kernel(held, right_side, first, second, total):
    odd, _ = first_axis_odd()

    def store(hop, other_hop, value):
        store_turned((first, second), lax.rem(other_hop // 2 + odd, 2), lax.rem(other_hop, 2), value)

    product_by_hop(held, right_side, total, 0, store)


def settle_kernel(own_first, own_second, first_free, first_joined, second_free, second_joined, *outs):
    keep, far, near, after = outs
    odd, other_odd = first_axis_odd()
    sums = own_first[...] + first_free[...] + second_joined[...], own_second[...] + first_joined[...] + second_free[...]
    for turn in range(2):

        @pl.when(odd == turn)
        def _(turn=turn):
            blocks = [sums[(hop // 2 + turn) % 2][hop % 2] for hop in range(RING)]
            keep[...], far[...] = blocks[0], blocks[2]
            for other_turn in range(2):

                @pl.when(other_odd == other_turn)
                def _(other_turn=other_turn):
                    near[...], after[...] = blocks[1 + 2 * other_turn], blocks[3 - 2 * other_turn]


def material_gradient(eliminated, kernel_coef, p_speed, s_speed, density):
    norming = 1.0 / jnp.sqrt(jnp.float32(SOURCES))
    fwd_real, fwd_imag, adj_real, adj_imag = (eliminated[:, at * SOURCES : (at + 1) * SOURCES] for at in range(4))
    k_lambda = jnp.sum(fwd_real * adj_real - fwd_imag * adj_imag, axis=1) * norming
    k_mu = jnp.sum(fwd_real * adj_imag + fwd_imag * adj_real, axis=1) * norming
    k_rho = jnp.sum(fwd_real * adj_real + fwd_imag * adj_imag, axis=1) * norming
    grad_lambda = kernel_coef[0] * k_lambda
    grad_mu = kernel_coef[1] * k_mu
    grad_rho = kernel_coef[2] * k_rho
    first_out = 2.0 * density * p_speed * grad_lambda
    second_out = 2.0 * density * s_speed * (grad_mu - 2.0 * grad_lambda)
    third_out = (
        (p_speed * p_speed - 2.0 * s_speed * s_speed) * grad_lambda
        + s_speed * s_speed * grad_mu
        + grad_rho
    )
    return jnp.stack([first_out, second_out, third_out])


def partner(at, way):
    return (at + 2) % RING if way == 2 else (at + 1 + 2 * ((at + way) % 2)) % RING


def swap_cores(value):
    return lax.ppermute(value, "row", [(i, i ^ 1) for i in range(2 * RING)])


def move_x(value, way):
    return lax.ppermute(value, "row", [(i, 2 * partner(i // 2, way) + i % 2) for i in range(2 * RING)])


def move_by_core(value, phase, way):
    pairs = []
    for former in range(2 * RING**3):
        row, y, z = former // RING**2, former // RING % RING, former % RING
        if (row + phase) % 2:
            z = partner(z, way)
        else:
            y = partner(y, way)
        pairs.append((former, (row * RING + y) * RING + z))
    return lax.ppermute(value, ("row", "col"), pairs)


def params(mebibytes, **more):
    return pltpu.CompilerParams(vmem_limit_bytes=mebibytes << 20, **more)


SMEM = pl.BlockSpec(memory_space=pltpu.SMEM)
VMEM = pl.BlockSpec(memory_space=pltpu.VMEM)
ANY = pl.BlockSpec(memory_space=pl.ANY)


def per_device(
    leaf_source,
    leaf_inv,
    leaf_low,
    child_count,
    child_owner,
    child_slot,
    parent_source,
    parent_inv,
    kernel_coef,
    p_speed,
    s_speed,
    density,
):
    devices = lax.axis_size("row") * lax.axis_size("col")
    owned = parent_source.shape[1]
    width = 2 * parent_source.shape[2]
    contrib = child_slot.shape[1]
    position = jnp.arange(contrib, dtype=jnp.int32)
    owner = jnp.where(position[None, :] < child_count[:, None], child_owner[:, :, 0], -1)

    outgoing = pl.pallas_call(
        leaf_kernel,
        out_shape=jax.ShapeDtypeStruct((devices * CAPACITY * width // LANES, LANES), F32),
        in_specs=[SMEM] + [ANY] * 4,
        out_specs=VMEM,
        scratch_shapes=[
            pltpu.VMEM((1, contrib), jnp.int32),
            pltpu.VMEM((2,) + leaf_source.shape[2:], F32),
            pltpu.VMEM(leaf_inv.shape[1:], F32),
            pltpu.VMEM(leaf_low.shape[1:], F32),
            pltpu.SemaphoreType.DMA((5,)),
        ],
        compiler_params=params(60),
        name="leaf",
    )(child_count, child_owner.reshape(devices, 1, contrib), leaf_source[:, 0], leaf_inv[0], leaf_low[0])
    rows, depth = parent_inv.shape[1:]
    block = rows // 8
    block_spec = pl.BlockSpec((2, block, depth), lambda i: (0, i, 0))
    units_shape = jax.ShapeDtypeStruct((UNITS, 2, 2, owned, depth // RING), BF16)
    units, token = pl.pallas_call(
        split_kernel,
        out_shape=[units_shape, jax.ShapeDtypeStruct((8, LANES), F32)],
        grid=(rows // block,),
        in_specs=[block_spec, ANY],
        out_specs=[pl.BlockSpec(units_shape.shape, lambda i: (0,) * 5), pl.BlockSpec((8, LANES), lambda i: (0, 0))],
        compiler_params=params(60),
        cost_estimate=pl.CostEstimate(flops=4 * rows * depth, bytes_accessed=16 * rows * depth, transcendentals=0),
        name="split",
    )(parent_inv, outgoing)
    placing = pl.pallas_call(
        placing_kernel,
        out_shape=jax.ShapeDtypeStruct((CAPACITY, devices, owned), BF16),
        in_specs=[VMEM] * 2 + [ANY],
        out_specs=VMEM,
        compiler_params=params(16),
        cost_estimate=pl.CostEstimate(flops=2 * devices * 512 * 512, bytes_accessed=1 << 20, transcendentals=0),
        name="placing",
    )(owner, child_slot, token)
    arrived = lax.all_to_all(
        outgoing.reshape(devices, -1, LANES), ("row", "col"), split_axis=0, concat_axis=0, tiled=True
    )
    assembled = pl.pallas_call(
        extend_kernel,
        out_shape=jax.ShapeDtypeStruct((owned, width), F32),
        in_specs=[VMEM] * 3,
        out_specs=VMEM,
        compiler_params=params(16),
        name="extend",
    )(placing, arrived.reshape(outgoing.shape), parent_source)

    other = swap_cores(assembled)
    hops = [move_x(assembled, way) for way in range(3)]
    swapped = [swap_cores(value) for value in hops]

    two = jax.ShapeDtypeStruct((2, owned, width), F32)

    total = pltpu.VMEM((RING * owned, width), F32)

    def cost(blocks):
        return pl.CostEstimate(flops=blocks * 6 * rows * depth * width, bytes_accessed=1 << 20, transcendentals=0)

    right_side, first, second, held = pl.pallas_call(
        far_kernel,
        out_shape=[jax.ShapeDtypeStruct((4, depth, width), BF16), two, two, units_shape],
        in_specs=[ANY] + [VMEM] * 8,
        out_specs=[VMEM] * 4,
        scratch_shapes=[pltpu.SemaphoreType.DMA((RING * RING,)), total],
        compiler_params=params(33),
        name="far",
    )(units, assembled, other, *hops, *swapped)
    got_first, got_second = move_by_core(first, 0, 0), move_by_core(second, 0, 1)

    def near(way, after):
        return pl.pallas_call(
            functools.partial(near_kernel, way),
            out_shape=[two] * 2,
            in_specs=[VMEM] * 2 + [ANY],
            out_specs=[VMEM] * 2,
            scratch_shapes=[total],
            compiler_params=params(36),
            cost_estimate=cost(1),
            name="near",
        )(held, right_side, after)

    first_free, first_joined = near(0, first)
    second_free, second_joined = near(1, first_joined)
    first_free, second_free = move_by_core(first_free, 0, 0), move_by_core(second_free, 0, 1)
    first_joined = move_by_core(first_joined + got_second, 0, 0)
    second_joined = move_by_core(second_joined + got_first, 0, 1)
    own = pl.pallas_call(
        own_kernel,
        out_shape=[two] * 2,
        in_specs=[VMEM] * 2,
        out_specs=[VMEM] * 2,
        scratch_shapes=[total],
        compiler_params=params(36),
        cost_estimate=cost(1),
        name="own",
    )(held, right_side)
    keep, far, closest, after = pl.pallas_call(
        settle_kernel,
        out_shape=[jax.ShapeDtypeStruct((owned, width), F32)] * 4,
        in_specs=[VMEM] * 6,
        out_specs=[VMEM] * 4,
        compiler_params=params(16),
        name="settle",
    )(*own, first_free, first_joined, second_free, second_joined)
    eliminated = keep + move_by_core(far, 1, 2) + move_by_core(closest, 1, 0) + move_by_core(after, 1, 1)
    return material_gradient(eliminated, kernel_coef, p_speed, s_speed, density)


def solution(mesh):
    return jax.shard_map(
        per_device,
        mesh=mesh,
        in_specs=(
            P(None, ("row", "col"), None, None),
            P(("row", "col"), None, None, None),
            P(("row", "col"), None, None, None),
            P(),
            P(),
            P(),
            P(None, ("row", "col"), None),
            P(None, "row", "col"),
            P(None, ("row", "col")),
            P(("row", "col")),
            P(("row", "col")),
            P(("row", "col")),
        ),
        out_specs=P(None, ("row", "col")),
        check_vma=False,
    )
```

```python
import functools

import jax
import jax.numpy as jnp
from jax import lax
from jax.experimental import pallas as pl
from jax.experimental.pallas import tpu as pltpu
from jax.sharding import PartitionSpec as P

SOURCES = 128
CAPACITY = 6
LANES = 128
RING = 4
F32 = jnp.float32
BF16 = jnp.bfloat16


def halves(value):
    high = value.astype(BF16)
    return high, (value - high.astype(F32)).astype(BF16)


def dot(left, right, dims=((1,), (0,))):
    return lax.dot_general(left, right, (dims, ((), ())), preferred_element_type=F32)


def left_parts(real_part, imag_part):
    real_high, real_low = halves(real_part)
    imag_high, imag_low = halves(imag_part)
    return jnp.concatenate([real_high, imag_high, real_high, imag_high, real_low, imag_low], axis=1)


def turned(value, part_width):
    parts = [value[:, at : at + part_width] for at in range(0, value.shape[1], part_width)]
    return jnp.concatenate(
        [part for at in range(0, len(parts), 2) for part in (-parts[at + 1], parts[at])], axis=1
    )


def right_parts(value):
    high, low = halves(value)
    turned_high, turned_low = (turned(part, value.shape[1] // 2) for part in (high, low))
    return jnp.concatenate([high, turned_high, low, turned_low, high, turned_high], axis=0)


def whereabouts():
    row, col = lax.axis_index("row"), lax.axis_index("col")
    return row * lax.axis_size("col") + col, row // 2, lax.rem(row, 2), col // RING, lax.rem(col, RING)


def running_count(mask):
    length = mask.shape[1]
    former = lax.broadcasted_iota(jnp.int32, (length, length), 0)
    latter = lax.broadcasted_iota(jnp.int32, (length, length), 1)
    upto = jnp.where(former <= latter, 1.0, 0.0).astype(BF16)
    return dot(mask.astype(BF16), upto)


def leaf_kernel(
    count_ref, owner_hbm, source_hbm, inv_hbm, low_hbm, out_hbm, owner_ref, source_ref, inv_ref, low_ref, split_ref, out_ref, sems
):
    devices, contrib = owner_hbm.shape[0], owner_ref.shape[1]
    myself = whereabouts()[0]
    pivots, breadth = inv_ref.shape[1], source_ref.shape[2]
    groups = 2 * breadth // LANES
    half = pivots // 2

    def some(former, latter, *at):
        return former.at[at], latter.at[at]

    copies = [
        pltpu.make_async_copy(former, latter, sems.at[i])
        for i, (former, latter) in enumerate(
            (
                (owner_hbm.at[myself], owner_ref),
                (low_hbm, low_ref),
                some(source_hbm, source_ref, slice(None), pl.ds(0, half)),
                some(inv_hbm, inv_ref, slice(None), pl.ds(0, half)),
                some(source_hbm, source_ref, slice(None), pl.ds(half, half)),
                some(inv_hbm, inv_ref, slice(None), pl.ds(half, half)),
                some(source_hbm, source_ref, slice(None), pl.ds(pivots, contrib)),
            )
        )
    ]
    for copy in copies:
        copy.start()
    copies[0].wait()
    names = lax.broadcasted_iota(jnp.int32, (devices, contrib), 0)
    position = lax.broadcasted_iota(jnp.int32, (devices, contrib), 1)
    chosen = jnp.where((names == owner_ref[...]) & (position < count_ref[myself]), 1.0, 0.0)
    rank = running_count(chosen) * chosen
    copies[1].wait()
    for part in range(2):
        split_ref[0, part], split_ref[1, part] = halves(low_ref[part])
    copies[2].wait()
    copies[3].wait()
    upper_source = jnp.concatenate([source_ref[0, :half], source_ref[1, :half]], axis=1)
    upper = dot(
        left_parts(inv_ref[0, :half, :half], inv_ref[1, :half, :half]), right_parts(upper_source)
    )
    copies[4].wait()
    copies[5].wait()
    pivot_source = jnp.concatenate([source_ref[0, :pivots], source_ref[1, :pivots]], axis=1)
    lower = dot(left_parts(inv_ref[0, half:], inv_ref[1, half:]), right_parts(pivot_source))
    pivot_part = right_parts(jnp.concatenate([upper, lower], axis=0))
    high, low = [split_ref[0, part] for part in range(2)], [split_ref[1, part] for part in range(2)]
    eliminated = dot(jnp.concatenate(high + high + low, axis=1), pivot_part)
    copies[6].wait()
    update = jnp.concatenate([source_ref[0, pivots:], source_ref[1, pivots:]], axis=1) - eliminated
    high, low = halves(update)
    both = jnp.concatenate([high, low], axis=0)
    share = devices // 2
    outs = []
    for i in range(2):
        some_rank = rank[i * share : (i + 1) * share]
        pick = jnp.concatenate(
            [jnp.where(some_rank == k + 1.0, 1.0, 0.0).astype(BF16) for k in range(CAPACITY)], axis=0
        )
        rows = dot(jnp.concatenate([pick, pick], axis=1), both)
        first = i * share * CAPACITY * groups
        for k in range(CAPACITY):
            for g in range(groups):
                at = (g % 2) * breadth + g // 2 * LANES
                out_ref[pl.ds(first + k * groups + g, share, stride=CAPACITY * groups), :] = rows[
                    k * share : (k + 1) * share, at : at + LANES
                ]
        span = pl.ds(first, share * CAPACITY * groups)
        outs.append(pltpu.make_async_copy(out_ref.at[span], out_hbm.at[span], sems.at[len(copies) + i]))
        outs[i].start()
    for copy in outs:
        copy.wait()


def placing_kernel(owner_ref, slot_ref, token_hbm, out_ref):
    del token_hbm
    devices = owner_ref.shape[0]
    owned = out_ref.shape[2]
    mine = jnp.where(owner_ref[...] == whereabouts()[0], 1.0, 0.0)
    rank = running_count(mine) * mine
    slots = slot_ref[...].astype(F32) + 1.0
    rows = lax.broadcasted_iota(jnp.int32, (devices, owned), 1).astype(F32) + 1.0
    for k in range(CAPACITY):
        slot = jnp.sum(jnp.where(rank == k + 1.0, slots, 0.0), axis=1, keepdims=True)
        out_ref[k] = jnp.where(slot == rows, 1.0, 0.0).astype(BF16)


def extend_kernel(placing_ref, arrived_ref, parent_ref, out_ref):
    devices = placing_ref.shape[1]
    groups = out_ref.shape[1] // LANES
    for g in range(groups):
        total = parent_ref[g % 2, :, g // 2 * LANES : (g // 2 + 1) * LANES]
        for k in range(CAPACITY):
            rows = arrived_ref[pl.ds(k * groups + g, devices, stride=CAPACITY * groups), :]
            high, low = halves(rows)
            total += dot(placing_ref[k], high, ((0,), (0,)))
            total += dot(placing_ref[k], low, ((0,), (0,)))
        out_ref[:, g * LANES : (g + 1) * LANES] = total


def first_unit(band, strip=0):
    return 2 * band * (band + 1) + strip * (band + 1)


UNITS = first_unit(RING)


def split_kernel(value_ref, after_hbm, out_ref, token_ref):
    del after_hbm
    token_ref[...] = jnp.zeros_like(token_ref)
    step = pl.program_id(0)
    rows, columns = out_ref.shape[3:]
    strips = value_ref.shape[1] // rows
    steps = RING // strips
    for band in range(RING):

        @pl.when(step // steps == band)
        def _(band=band):
            for j in range(strips):
                strip = lax.rem(step, steps) * strips + j
                for piece in range(band + 1):
                    for part in range(2):
                        value = value_ref[part, j * rows : (j + 1) * rows, piece * columns : (piece + 1) * columns]
                        high, low = halves(value)
                        out_ref[first_unit(band, strip) + piece, 0, part] = high
                        out_ref[first_unit(band, strip) + piece, 1, part] = low


def piece_product(held, right_ref, units, piece):
    depth = held.shape[4]

    def rows(kind, part):
        return jnp.concatenate([held[unit, kind, part] for unit in units], axis=0)

    high, low = ([rows(kind, part) for part in range(2)] for kind in range(2))
    right = [right_ref[kind, pl.ds(pl.multiple_of(piece * depth, depth), depth)] for kind in range(4)]
    return dot(
        jnp.concatenate([high[0], high[1], high[0], high[1], low[0], low[1]], axis=1),
        jnp.concatenate([right[0], right[1], right[2], right[3], right[0], right[1]], axis=0),
    )


def hop_from(own, index):
    return lax.rem(index - own + RING, RING)


def product_by_hop(held, right_ref, total, hop, store):
    owned = held.shape[3]
    _, _, own_core, own_y, own_z = whereabouts()

    @pl.when(own_core == 0)
    def _():
        band = lax.rem(own_y + hop, RING)
        total[...] = jnp.zeros_like(total)

        def add(piece, carry):
            units = [first_unit(band, strip) + piece for strip in range(RING)]
            total[...] += piece_product(held, right_ref, units, piece)
            return carry

        lax.fori_loop(0, band + 1, add, 0)
        for strip in range(RING):
            store(hop, hop_from(own_z, strip), total[strip * owned : (strip + 1) * owned])

    @pl.when(own_core == 1)
    def _():
        strip = lax.rem(own_z + hop, RING)
        for piece in range(RING):
            units = [first_unit(band, strip) + piece for band in range(piece, RING)]
            value = piece_product(held, right_ref, units, piece)
            if piece:
                total[piece * owned :] += value
            else:
                total[...] = value
        for band in range(RING):
            store(hop, hop_from(own_y, band), total[band * owned : (band + 1) * owned])


def first_axis_odd():
    _, _, own_core, own_y, own_z = whereabouts()
    odd_y, odd_z = lax.rem(own_y, 2), lax.rem(own_z, 2)
    return jnp.where(own_core == 0, odd_y, odd_z), jnp.where(own_core == 0, odd_z, odd_y)


def store_turned(refs, which, slot, value):
    for at, ref in enumerate(refs):

        @pl.when(which == at)
        def _(ref=ref):
            ref[slot] = value


def kinds_of(value):
    high, low = halves(value)
    return high, turned(high, SOURCES), low, turned(low, SOURCES)


def load_kernel(units_hbm, own_ref, other_ref, far_ref, filled, held, far_out, sem):
    copy = pltpu.make_async_copy(units_hbm, held, sem)
    copy.start()
    for at, ref in enumerate((own_ref, other_ref, far_ref)):
        for kind, value in enumerate(kinds_of(ref[...])):
            filled[kind, at] = value
    far_out[...] = far_ref[...]
    copy.wait()


def far_kernel(filled, held, near_ref, next_ref, near2_ref, next2_ref, far2_ref, right_side, first, second, total):
    owned = near_ref.shape[0]
    _, own_x, own_core, _, _ = whereabouts()
    odd_x = lax.rem(own_x, 2)
    odd, _ = first_axis_odd()

    def rows_of(hop, core):
        return pl.ds(pl.multiple_of((lax.rem(own_x + hop, RING) * 2 + core) * owned, owned), owned)

    for at, place in enumerate((rows_of(0, own_core), rows_of(0, 1 - own_core), rows_of(2, own_core))):
        for kind in range(4):
            right_side[kind, place, :] = filled[kind, at]
    for hop, ref, core in (
        (1 + 2 * odd_x, near_ref, own_core), (3 - 2 * odd_x, next_ref, own_core), (1 + 2 * odd_x, near2_ref, 1 - own_core),
        (3 - 2 * odd_x, next2_ref, 1 - own_core), (2, far2_ref, 1 - own_core),
    ):
        for kind, value in enumerate(kinds_of(ref[...])):
            right_side[kind, rows_of(hop, core), :] = value

    def store(hop, other_hop, value):
        store_turned((first, second), lax.rem(other_hop // 2 + odd, 2), lax.rem(other_hop, 2), value)

    product_by_hop(held, right_side, total, 2, store)


def near_kernel(way, held, right_side, after_any, free, joined, total):
    del after_any
    odd, _ = first_axis_odd()
    hop = 1 + 2 * lax.rem(way + odd, 2)

    def store(hop, other_hop, value):
        store_turned((free, joined), jnp.where(other_hop // 2 == hop // 2, 1, 0), lax.rem(other_hop, 2), value)

    product_by_hop(held, right_side, total, hop, store)


def own_kernel(held, right_side, first, second, total):
    odd, _ = first_axis_odd()

    def store(hop, other_hop, value):
        store_turned((first, second), lax.rem(other_hop // 2 + odd, 2), lax.rem(other_hop, 2), value)

    product_by_hop(held, right_side, total, 0, store)


def settle_kernel(own_first, own_second, first_free, first_joined, second_free, second_joined, *outs):
    keep, far, near, after = outs
    odd, other_odd = first_axis_odd()
    sums = own_first[...] + first_free[...] + second_joined[...], own_second[...] + first_joined[...] + second_free[...]
    for turn in range(2):

        @pl.when(odd == turn)
        def _(turn=turn):
            blocks = [sums[(hop // 2 + turn) % 2][hop % 2] for hop in range(RING)]
            keep[...], far[...] = blocks[0], blocks[2]
            for other_turn in range(2):

                @pl.when(other_odd == other_turn)
                def _(other_turn=other_turn):
                    near[...], after[...] = blocks[1 + 2 * other_turn], blocks[3 - 2 * other_turn]


def material_gradient(eliminated, kernel_coef, p_speed, s_speed, density):
    norming = 1.0 / jnp.sqrt(jnp.float32(SOURCES))
    fwd_real, fwd_imag, adj_real, adj_imag = (eliminated[:, at * SOURCES : (at + 1) * SOURCES] for at in range(4))
    k_lambda = jnp.sum(fwd_real * adj_real - fwd_imag * adj_imag, axis=1) * norming
    k_mu = jnp.sum(fwd_real * adj_imag + fwd_imag * adj_real, axis=1) * norming
    k_rho = jnp.sum(fwd_real * adj_real + fwd_imag * adj_imag, axis=1) * norming
    grad_lambda = kernel_coef[0] * k_lambda
    grad_mu = kernel_coef[1] * k_mu
    grad_rho = kernel_coef[2] * k_rho
    first_out = 2.0 * density * p_speed * grad_lambda
    second_out = 2.0 * density * s_speed * (grad_mu - 2.0 * grad_lambda)
    third_out = (
        (p_speed * p_speed - 2.0 * s_speed * s_speed) * grad_lambda
        + s_speed * s_speed * grad_mu
        + grad_rho
    )
    return jnp.stack([first_out, second_out, third_out])


def partner(at, way):
    return (at + 2) % RING if way == 2 else (at + 1 + 2 * ((at + way) % 2)) % RING


def swap_cores(value):
    return lax.ppermute(value, "row", [(i, i ^ 1) for i in range(2 * RING)])


def move_x(value, way):
    return lax.ppermute(value, "row", [(i, 2 * partner(i // 2, way) + i % 2) for i in range(2 * RING)])


def move_by_core(value, phase, way):
    pairs = []
    for former in range(2 * RING**3):
        row, y, z = former // RING**2, former // RING % RING, former % RING
        if (row + phase) % 2:
            z = partner(z, way)
        else:
            y = partner(y, way)
        pairs.append((former, (row * RING + y) * RING + z))
    return lax.ppermute(value, ("row", "col"), pairs)


def params(mebibytes, **more):
    return pltpu.CompilerParams(vmem_limit_bytes=mebibytes << 20, **more)


SMEM = pl.BlockSpec(memory_space=pltpu.SMEM)
VMEM = pl.BlockSpec(memory_space=pltpu.VMEM)
ANY = pl.BlockSpec(memory_space=pl.ANY)


def per_device(
    leaf_source,
    leaf_inv,
    leaf_low,
    child_count,
    child_owner,
    child_slot,
    parent_source,
    parent_inv,
    kernel_coef,
    p_speed,
    s_speed,
    density,
):
    devices = lax.axis_size("row") * lax.axis_size("col")
    owned = parent_source.shape[1]
    width = 2 * parent_source.shape[2]
    contrib = child_slot.shape[1]
    position = jnp.arange(contrib, dtype=jnp.int32)
    owner = jnp.where(position[None, :] < child_count[:, None], child_owner[:, :, 0], -1)

    outgoing_shape = (devices * CAPACITY * width // LANES, LANES)
    outgoing = pl.pallas_call(
        leaf_kernel,
        out_shape=jax.ShapeDtypeStruct(outgoing_shape, F32),
        in_specs=[SMEM] + [ANY] * 4,
        out_specs=ANY,
        scratch_shapes=[
            pltpu.VMEM((1, contrib), jnp.int32),
            pltpu.VMEM((2,) + leaf_source.shape[2:], F32),
            pltpu.VMEM(leaf_inv.shape[1:], F32),
            pltpu.VMEM(leaf_low.shape[1:], F32),
            pltpu.VMEM((2,) + leaf_low.shape[1:], BF16),
            pltpu.VMEM(outgoing_shape, F32),
            pltpu.SemaphoreType.DMA((9,)),
        ],
        compiler_params=params(60),
        name="leaf",
    )(child_count, child_owner.reshape(devices, 1, contrib), leaf_source[:, 0], leaf_inv[0], leaf_low[0])
    rows, depth = parent_inv.shape[1:]
    block = rows // 8
    block_spec = pl.BlockSpec((2, block, depth), lambda i: (0, i, 0))
    units_shape = jax.ShapeDtypeStruct((UNITS, 2, 2, owned, depth // RING), BF16)
    units, token = pl.pallas_call(
        split_kernel,
        out_shape=[units_shape, jax.ShapeDtypeStruct((8, LANES), F32)],
        grid=(rows // block,),
        in_specs=[block_spec, ANY],
        out_specs=[pl.BlockSpec(units_shape.shape, lambda i: (0,) * 5), pl.BlockSpec((8, LANES), lambda i: (0, 0))],
        compiler_params=params(60),
        cost_estimate=pl.CostEstimate(flops=4 * rows * depth, bytes_accessed=16 * rows * depth, transcendentals=0),
        name="split",
    )(parent_inv, outgoing)
    placing = pl.pallas_call(
        placing_kernel,
        out_shape=jax.ShapeDtypeStruct((CAPACITY, devices, owned), BF16),
        in_specs=[VMEM] * 2 + [ANY],
        out_specs=VMEM,
        compiler_params=params(16),
        cost_estimate=pl.CostEstimate(flops=2 * devices * 512 * 512, bytes_accessed=1 << 20, transcendentals=0),
        name="placing",
    )(owner, child_slot, token)
    arrived = lax.all_to_all(
        outgoing.reshape(devices, -1, LANES), ("row", "col"), split_axis=0, concat_axis=0, tiled=True
    )
    assembled = pl.pallas_call(
        extend_kernel,
        out_shape=jax.ShapeDtypeStruct((owned, width), F32),
        in_specs=[VMEM] * 3,
        out_specs=VMEM,
        compiler_params=params(16),
        name="extend",
    )(placing, arrived.reshape(outgoing.shape), parent_source)

    other = swap_cores(assembled)
    hops = [move_x(assembled, way) for way in range(3)]
    filled, held, hops[2] = pl.pallas_call(
        load_kernel,
        out_shape=[
            jax.ShapeDtypeStruct((4, 3, owned, width), BF16), units_shape, jax.ShapeDtypeStruct((owned, width), F32)
        ],
        in_specs=[ANY] + [VMEM] * 3,
        out_specs=[VMEM] * 3,
        scratch_shapes=[pltpu.SemaphoreType.DMA],
        compiler_params=params(40),
        name="load",
    )(units, assembled, other, hops[2])
    swapped = [swap_cores(value) for value in hops]

    two = jax.ShapeDtypeStruct((2, owned, width), F32)

    total = pltpu.VMEM((RING * owned, width), F32)

    def cost(blocks):
        return pl.CostEstimate(flops=blocks * rows * depth * width // 8, bytes_accessed=1 << 18, transcendentals=0)

    right_side, first, second = pl.pallas_call(
        far_kernel,
        out_shape=[jax.ShapeDtypeStruct((4, depth, width), BF16), two, two],
        in_specs=[VMEM] * 7,
        out_specs=[VMEM] * 3,
        scratch_shapes=[total],
        compiler_params=params(33),
        name="far",
    )(filled, held, *hops[:2], *swapped)
    got_first, got_second = move_by_core(first, 0, 0), move_by_core(second, 0, 1)

    def near(way, after):
        return pl.pallas_call(
            functools.partial(near_kernel, way),
            out_shape=[two] * 2,
            in_specs=[VMEM] * 2 + [ANY],
            out_specs=[VMEM] * 2,
            scratch_shapes=[total],
            compiler_params=params(36),
            cost_estimate=cost(1),
            name="near",
        )(held, right_side, after)

    first_free, first_joined = near(0, first)
    second_free, second_joined = near(1, first_joined)
    first_free, second_free = move_by_core(first_free, 0, 0), move_by_core(second_free, 0, 1)
    first_joined = move_by_core(first_joined + got_second, 0, 0)
    second_joined = move_by_core(second_joined + got_first, 0, 1)
    own = pl.pallas_call(
        own_kernel,
        out_shape=[two] * 2,
        in_specs=[VMEM] * 2,
        out_specs=[VMEM] * 2,
        scratch_shapes=[total],
        compiler_params=params(36),
        cost_estimate=cost(1),
        name="own",
    )(held, right_side)
    keep, far, closest, after = pl.pallas_call(
        settle_kernel,
        out_shape=[jax.ShapeDtypeStruct((owned, width), F32)] * 4,
        in_specs=[VMEM] * 6,
        out_specs=[VMEM] * 4,
        compiler_params=params(16),
        name="settle",
    )(*own, first_free, first_joined, second_free, second_joined)
    eliminated = keep + move_by_core(far, 1, 2) + move_by_core(closest, 1, 0) + move_by_core(after, 1, 1)
    return material_gradient(eliminated, kernel_coef, p_speed, s_speed, density)


def solution(mesh):
    return jax.shard_map(
        per_device,
        mesh=mesh,
        in_specs=(
            P(None, ("row", "col"), None, None),
            P(("row", "col"), None, None, None),
            P(("row", "col"), None, None, None),
            P(),
            P(),
            P(),
            P(None, ("row", "col"), None),
            P(None, "row", "col"),
            P(None, ("row", "col")),
            P(("row", "col")),
            P(("row", "col")),
            P(("row", "col")),
        ),
        out_specs=P(None, ("row", "col")),
        check_vma=False,
    )
```

```python
import functools

import jax
import jax.numpy as jnp
from jax import lax
from jax.experimental import pallas as pl
from jax.experimental.pallas import tpu as pltpu
from jax.sharding import PartitionSpec as P

SOURCES = 128
CAPACITY = 6
LANES = 128
RING = 4
F32 = jnp.float32
BF16 = jnp.bfloat16


def halves(value):
    high = value.astype(BF16)
    return high, (value - high.astype(F32)).astype(BF16)


def dot(left, right, dims=((1,), (0,))):
    return lax.dot_general(left, right, (dims, ((), ())), preferred_element_type=F32)


def left_parts(real_part, imag_part):
    real_high, real_low = halves(real_part)
    imag_high, imag_low = halves(imag_part)
    return jnp.concatenate([real_high, imag_high, real_high, imag_high, real_low, imag_low], axis=1)


def turned(value, part_width):
    parts = [value[:, at : at + part_width] for at in range(0, value.shape[1], part_width)]
    return jnp.concatenate(
        [part for at in range(0, len(parts), 2) for part in (-parts[at + 1], parts[at])], axis=1
    )


def right_parts(value):
    high, low = halves(value)
    turned_high, turned_low = (turned(part, value.shape[1] // 2) for part in (high, low))
    return jnp.concatenate([high, turned_high, low, turned_low, high, turned_high], axis=0)


def whereabouts():
    row, col = lax.axis_index("row"), lax.axis_index("col")
    return row * lax.axis_size("col") + col, row // 2, lax.rem(row, 2), col // RING, lax.rem(col, RING)


def running_count(mask):
    length = mask.shape[1]
    former = lax.broadcasted_iota(jnp.int32, (length, length), 0)
    latter = lax.broadcasted_iota(jnp.int32, (length, length), 1)
    upto = jnp.where(former <= latter, 1.0, 0.0).astype(BF16)
    return dot(mask.astype(BF16), upto)


def leaf_kernel(
    count_ref, owner_hbm, source_hbm, inv_hbm, low_hbm, out_hbm, owner_ref, source_ref, inv_ref, low_ref, split_ref, out_ref, sems
):
    devices, contrib = owner_hbm.shape[0], owner_ref.shape[1]
    myself = whereabouts()[0]
    pivots, breadth = inv_ref.shape[1], source_ref.shape[2]
    groups = 2 * breadth // LANES
    half = pivots // 2

    def some(former, latter, *at):
        return former.at[at], latter.at[at]

    copies = [
        pltpu.make_async_copy(former, latter, sems.at[i])
        for i, (former, latter) in enumerate(
            (
                (owner_hbm.at[myself], owner_ref),
                (low_hbm, low_ref),
                some(source_hbm, source_ref, slice(None), pl.ds(0, half)),
                some(inv_hbm, inv_ref, slice(None), pl.ds(0, half)),
                some(source_hbm, source_ref, slice(None), pl.ds(half, half)),
                some(inv_hbm, inv_ref, slice(None), pl.ds(half, half)),
                some(source_hbm, source_ref, slice(None), pl.ds(pivots, contrib)),
            )
        )
    ]
    for copy in copies:
        copy.start()
    copies[0].wait()
    names = lax.broadcasted_iota(jnp.int32, (devices, contrib), 0)
    position = lax.broadcasted_iota(jnp.int32, (devices, contrib), 1)
    chosen = jnp.where((names == owner_ref[...]) & (position < count_ref[myself]), 1.0, 0.0)
    rank = running_count(chosen) * chosen
    copies[1].wait()
    for part in range(2):
        split_ref[0, part], split_ref[1, part] = halves(low_ref[part])
    copies[2].wait()
    copies[3].wait()
    upper_source = jnp.concatenate([source_ref[0, :half], source_ref[1, :half]], axis=1)
    upper = dot(
        left_parts(inv_ref[0, :half, :half], inv_ref[1, :half, :half]), right_parts(upper_source)
    )
    copies[4].wait()
    copies[5].wait()
    pivot_source = jnp.concatenate([source_ref[0, :pivots], source_ref[1, :pivots]], axis=1)
    lower = dot(left_parts(inv_ref[0, half:], inv_ref[1, half:]), right_parts(pivot_source))
    pivot_part = right_parts(jnp.concatenate([upper, lower], axis=0))
    high, low = [split_ref[0, part] for part in range(2)], [split_ref[1, part] for part in range(2)]
    eliminated = dot(jnp.concatenate(high + high + low, axis=1), pivot_part)
    copies[6].wait()
    update = jnp.concatenate([source_ref[0, pivots:], source_ref[1, pivots:]], axis=1) - eliminated
    high, low = halves(update)
    both = jnp.concatenate([high, low], axis=0)
    share = devices // 2
    outs = []
    for i in range(2):
        some_rank = rank[i * share : (i + 1) * share]
        pick = jnp.concatenate(
            [jnp.where(some_rank == k + 1.0, 1.0, 0.0).astype(BF16) for k in range(CAPACITY)], axis=0
        )
        rows = dot(jnp.concatenate([pick, pick], axis=1), both)
        first = i * share * CAPACITY * groups
        for k in range(CAPACITY):
            for g in range(groups):
                at = (g % 2) * breadth + g // 2 * LANES
                out_ref[pl.ds(first + k * groups + g, share, stride=CAPACITY * groups), :] = rows[
                    k * share : (k + 1) * share, at : at + LANES
                ]
        span = pl.ds(first, share * CAPACITY * groups)
        outs.append(pltpu.make_async_copy(out_ref.at[span], out_hbm.at[span], sems.at[len(copies) + i]))
        outs[i].start()
    for copy in outs:
        copy.wait()


def placing_kernel(owner_ref, slot_ref, token_hbm, out_ref):
    del token_hbm
    devices = owner_ref.shape[0]
    owned = out_ref.shape[2]
    mine = jnp.where(owner_ref[...] == whereabouts()[0], 1.0, 0.0)
    rank = running_count(mine) * mine
    slots = slot_ref[...].astype(F32) + 1.0
    rows = lax.broadcasted_iota(jnp.int32, (devices, owned), 1).astype(F32) + 1.0
    for k in range(CAPACITY):
        slot = jnp.sum(jnp.where(rank == k + 1.0, slots, 0.0), axis=1, keepdims=True)
        out_ref[k] = jnp.where(slot == rows, 1.0, 0.0).astype(BF16)


def extend_kernel(placing_ref, arrived_ref, parent_ref, out_ref):
    devices = placing_ref.shape[1]
    groups = out_ref.shape[1] // LANES
    for g in range(groups):
        total = parent_ref[g % 2, :, g // 2 * LANES : (g // 2 + 1) * LANES]
        for k in range(CAPACITY):
            rows = arrived_ref[pl.ds(k * groups + g, devices, stride=CAPACITY * groups), :]
            high, low = halves(rows)
            total += dot(placing_ref[k], high, ((0,), (0,)))
            total += dot(placing_ref[k], low, ((0,), (0,)))
        out_ref[:, g * LANES : (g + 1) * LANES] = total


def first_unit(band, strip=0):
    return 2 * band * (band + 1) + strip * (band + 1)


UNITS = first_unit(RING)


def split_kernel(value_ref, after_hbm, out_ref, token_ref):
    del after_hbm
    token_ref[...] = jnp.zeros_like(token_ref)
    step = pl.program_id(0)
    rows, columns = out_ref.shape[3:]
    strips = value_ref.shape[1] // rows
    steps = RING // strips
    for band in range(RING):

        @pl.when(step // steps == band)
        def _(band=band):
            for j in range(strips):
                strip = lax.rem(step, steps) * strips + j
                for piece in range(band + 1):
                    for part in range(2):
                        value = value_ref[part, j * rows : (j + 1) * rows, piece * columns : (piece + 1) * columns]
                        high, low = halves(value)
                        out_ref[first_unit(band, strip) + piece, 0, part] = high
                        out_ref[first_unit(band, strip) + piece, 1, part] = low


def piece_product(held, right_ref, units, piece):
    depth = held.shape[4]

    def rows(kind, part):
        return jnp.concatenate([held[unit, kind, part] for unit in units], axis=0)

    high, low = ([rows(kind, part) for part in range(2)] for kind in range(2))
    right = [right_ref[kind, pl.ds(pl.multiple_of(piece * depth, depth), depth)] for kind in range(4)]
    return dot(
        jnp.concatenate([high[0], high[1], high[0], high[1], low[0], low[1]], axis=1),
        jnp.concatenate([right[0], right[1], right[2], right[3], right[0], right[1]], axis=0),
    )


def hop_from(own, index):
    return lax.rem(index - own + RING, RING)


def product_by_hop(held, right_ref, total, hop, store):
    owned = held.shape[3]
    _, _, own_core, own_y, own_z = whereabouts()

    @pl.when(own_core == 0)
    def _():
        band = lax.rem(own_y + hop, RING)
        total[...] = jnp.zeros_like(total)

        def add(piece, carry):
            units = [first_unit(band, strip) + piece for strip in range(RING)]
            total[...] += piece_product(held, right_ref, units, piece)
            return carry

        lax.fori_loop(0, band + 1, add, 0)
        for strip in range(RING):
            store(hop, hop_from(own_z, strip), total[strip * owned : (strip + 1) * owned])

    @pl.when(own_core == 1)
    def _():
        strip = lax.rem(own_z + hop, RING)
        for piece in range(RING):
            units = [first_unit(band, strip) + piece for band in range(piece, RING)]
            value = piece_product(held, right_ref, units, piece)
            if piece:
                total[piece * owned :] += value
            else:
                total[...] = value
        for band in range(RING):
            store(hop, hop_from(own_y, band), total[band * owned : (band + 1) * owned])


def first_axis_odd():
    _, _, own_core, own_y, own_z = whereabouts()
    odd_y, odd_z = lax.rem(own_y, 2), lax.rem(own_z, 2)
    return jnp.where(own_core == 0, odd_y, odd_z), jnp.where(own_core == 0, odd_z, odd_y)


def store_turned(refs, which, slot, value):
    for at, ref in enumerate(refs):

        @pl.when(which == at)
        def _(ref=ref):
            ref[slot] = value


def kinds_of(value):
    high, low = halves(value)
    return high, turned(high, SOURCES), low, turned(low, SOURCES)


def load_kernel(units_hbm, own_ref, other_ref, far_ref, filled, held, far_out, sem):
    copy = pltpu.make_async_copy(units_hbm, held, sem)
    copy.start()
    for at, ref in enumerate((own_ref, other_ref, far_ref)):
        for kind, value in enumerate(kinds_of(ref[...])):
            filled[kind, at] = value
    far_out[...] = far_ref[...]
    copy.wait()


def far_kernel(filled, held, near_ref, next_ref, near2_ref, next2_ref, far2_ref, right_side, first, second, total):
    owned = near_ref.shape[0]
    _, own_x, own_core, _, _ = whereabouts()
    odd_x = lax.rem(own_x, 2)
    odd, _ = first_axis_odd()

    def rows_of(hop, core):
        return pl.ds(pl.multiple_of((lax.rem(own_x + hop, RING) * 2 + core) * owned, owned), owned)

    for at, place in enumerate((rows_of(0, own_core), rows_of(0, 1 - own_core), rows_of(2, own_core))):
        for kind in range(4):
            right_side[kind, place, :] = filled[kind, at]
    for hop, ref, core in (
        (1 + 2 * odd_x, near_ref, own_core), (3 - 2 * odd_x, next_ref, own_core), (1 + 2 * odd_x, near2_ref, 1 - own_core),
        (3 - 2 * odd_x, next2_ref, 1 - own_core), (2, far2_ref, 1 - own_core),
    ):
        for kind, value in enumerate(kinds_of(ref[...])):
            right_side[kind, rows_of(hop, core), :] = value

    def store(hop, other_hop, value):
        store_turned((first, second), lax.rem(other_hop // 2 + odd, 2), lax.rem(other_hop, 2), value)

    product_by_hop(held, right_side, total, 2, store)


def near_kernel(way, held, right_side, after_any, free, joined, total):
    del after_any
    odd, _ = first_axis_odd()
    hop = 1 + 2 * lax.rem(way + odd, 2)

    def store(hop, other_hop, value):
        store_turned((free, joined), jnp.where(other_hop // 2 == hop // 2, 1, 0), lax.rem(other_hop, 2), value)

    product_by_hop(held, right_side, total, hop, store)


def own_kernel(held, right_side, first, second, total):
    odd, _ = first_axis_odd()

    def store(hop, other_hop, value):
        store_turned((first, second), lax.rem(other_hop // 2 + odd, 2), lax.rem(other_hop, 2), value)

    product_by_hop(held, right_side, total, 0, store)


def settle_kernel(own_first, own_second, first_free, first_joined, second_free, second_joined, *outs):
    keep, far, near, after = outs
    odd, other_odd = first_axis_odd()
    sums = own_first[...] + first_free[...] + second_joined[...], own_second[...] + first_joined[...] + second_free[...]
    for turn in range(2):

        @pl.when(odd == turn)
        def _(turn=turn):
            blocks = [sums[(hop // 2 + turn) % 2][hop % 2] for hop in range(RING)]
            keep[...], far[...] = blocks[0], blocks[2]
            for other_turn in range(2):

                @pl.when(other_odd == other_turn)
                def _(other_turn=other_turn):
                    near[...], after[...] = blocks[1 + 2 * other_turn], blocks[3 - 2 * other_turn]


def gradient_kernel(keep, far, closest, after, coef, p_speed, s_speed, density, out):
    norming = SOURCES**-0.5
    whole = (keep[...] + far[...]) + (closest[...] + after[...])
    fwd_real, fwd_imag, adj_real, adj_imag = (whole[:, at * SOURCES : (at + 1) * SOURCES] for at in range(4))

    def over_sources(value):
        return jnp.sum(value.T, axis=0, keepdims=True) * norming

    real, imag = fwd_real * adj_real, fwd_imag * adj_imag
    grad_lambda = coef[0:1] * over_sources(real - imag)
    grad_mu = coef[1:2] * over_sources(fwd_real * adj_imag + fwd_imag * adj_real)
    grad_rho = coef[2:3] * over_sources(real + imag)
    p, s, rho = p_speed[...], s_speed[...], density[...]
    out[0:1] = 2.0 * rho * p * grad_lambda
    out[1:2] = 2.0 * rho * s * (grad_mu - 2.0 * grad_lambda)
    out[2:3] = (p * p - 2.0 * s * s) * grad_lambda + s * s * grad_mu + grad_rho


def partner(at, way):
    return (at + 2) % RING if way == 2 else (at + 1 + 2 * ((at + way) % 2)) % RING


def swap_cores(value):
    return lax.ppermute(value, "row", [(i, i ^ 1) for i in range(2 * RING)])


def move_x(value, way):
    return lax.ppermute(value, "row", [(i, 2 * partner(i // 2, way) + i % 2) for i in range(2 * RING)])


def move_by_core(value, phase, way):
    pairs = []
    for former in range(2 * RING**3):
        row, y, z = former // RING**2, former // RING % RING, former % RING
        if (row + phase) % 2:
            z = partner(z, way)
        else:
            y = partner(y, way)
        pairs.append((former, (row * RING + y) * RING + z))
    return lax.ppermute(value, ("row", "col"), pairs)


def params(mebibytes, **more):
    return pltpu.CompilerParams(vmem_limit_bytes=mebibytes << 20, **more)


SMEM = pl.BlockSpec(memory_space=pltpu.SMEM)
VMEM = pl.BlockSpec(memory_space=pltpu.VMEM)
ANY = pl.BlockSpec(memory_space=pl.ANY)


def per_device(
    leaf_source,
    leaf_inv,
    leaf_low,
    child_count,
    child_owner,
    child_slot,
    parent_source,
    parent_inv,
    kernel_coef,
    p_speed,
    s_speed,
    density,
):
    devices = lax.axis_size("row") * lax.axis_size("col")
    owned = parent_source.shape[1]
    width = 2 * parent_source.shape[2]
    contrib = child_slot.shape[1]
    position = jnp.arange(contrib, dtype=jnp.int32)
    owner = jnp.where(position[None, :] < child_count[:, None], child_owner[:, :, 0], -1)

    outgoing_shape = (devices * CAPACITY * width // LANES, LANES)
    outgoing = pl.pallas_call(
        leaf_kernel,
        out_shape=jax.ShapeDtypeStruct(outgoing_shape, F32),
        in_specs=[SMEM] + [ANY] * 4,
        out_specs=ANY,
        scratch_shapes=[
            pltpu.VMEM((1, contrib), jnp.int32),
            pltpu.VMEM((2,) + leaf_source.shape[2:], F32),
            pltpu.VMEM(leaf_inv.shape[1:], F32),
            pltpu.VMEM(leaf_low.shape[1:], F32),
            pltpu.VMEM((2,) + leaf_low.shape[1:], BF16),
            pltpu.VMEM(outgoing_shape, F32),
            pltpu.SemaphoreType.DMA((9,)),
        ],
        compiler_params=params(60),
        name="leaf",
    )(child_count, child_owner.reshape(devices, 1, contrib), leaf_source[:, 0], leaf_inv[0], leaf_low[0])
    rows, depth = parent_inv.shape[1:]
    block = rows // 8
    block_spec = pl.BlockSpec((2, block, depth), lambda i: (0, i, 0))
    units_shape = jax.ShapeDtypeStruct((UNITS, 2, 2, owned, depth // RING), BF16)
    units, token = pl.pallas_call(
        split_kernel,
        out_shape=[units_shape, jax.ShapeDtypeStruct((8, LANES), F32)],
        grid=(rows // block,),
        in_specs=[block_spec, ANY],
        out_specs=[pl.BlockSpec(units_shape.shape, lambda i: (0,) * 5), pl.BlockSpec((8, LANES), lambda i: (0, 0))],
        compiler_params=params(60),
        cost_estimate=pl.CostEstimate(flops=4 * rows * depth, bytes_accessed=16 * rows * depth, transcendentals=0),
        name="split",
    )(parent_inv, outgoing)
    placing = pl.pallas_call(
        placing_kernel,
        out_shape=jax.ShapeDtypeStruct((CAPACITY, devices, owned), BF16),
        in_specs=[VMEM] * 2 + [ANY],
        out_specs=VMEM,
        compiler_params=params(16),
        cost_estimate=pl.CostEstimate(flops=2 * devices * 512 * 512, bytes_accessed=1 << 20, transcendentals=0),
        name="placing",
    )(owner, child_slot, token)
    arrived = lax.all_to_all(
        outgoing.reshape(devices, -1, LANES), ("row", "col"), split_axis=0, concat_axis=0, tiled=True
    )
    assembled = pl.pallas_call(
        extend_kernel,
        out_shape=jax.ShapeDtypeStruct((owned, width), F32),
        in_specs=[VMEM] * 3,
        out_specs=VMEM,
        compiler_params=params(16),
        name="extend",
    )(placing, arrived.reshape(outgoing.shape), parent_source)

    other = swap_cores(assembled)
    hops = [move_x(assembled, way) for way in range(3)]
    filled, held, hops[2] = pl.pallas_call(
        load_kernel,
        out_shape=[
            jax.ShapeDtypeStruct((4, 3, owned, width), BF16), units_shape, jax.ShapeDtypeStruct((owned, width), F32)
        ],
        in_specs=[ANY] + [VMEM] * 3,
        out_specs=[VMEM] * 3,
        scratch_shapes=[pltpu.SemaphoreType.DMA],
        compiler_params=params(40),
        name="load",
    )(units, assembled, other, hops[2])
    swapped = [swap_cores(value) for value in hops]

    two = jax.ShapeDtypeStruct((2, owned, width), F32)

    total = pltpu.VMEM((RING * owned, width), F32)

    def cost(blocks):
        return pl.CostEstimate(flops=blocks * rows * depth * width // 8, bytes_accessed=1 << 18, transcendentals=0)

    right_side, first, second = pl.pallas_call(
        far_kernel,
        out_shape=[jax.ShapeDtypeStruct((4, depth, width), BF16), two, two],
        in_specs=[VMEM] * 7,
        out_specs=[VMEM] * 3,
        scratch_shapes=[total],
        compiler_params=params(33),
        name="far",
    )(filled, held, *hops[:2], *swapped)
    got_first, got_second = move_by_core(first, 0, 0), move_by_core(second, 0, 1)

    def near(way, after):
        return pl.pallas_call(
            functools.partial(near_kernel, way),
            out_shape=[two] * 2,
            in_specs=[VMEM] * 2 + [ANY],
            out_specs=[VMEM] * 2,
            scratch_shapes=[total],
            compiler_params=params(36),
            cost_estimate=cost(1),
            name="near",
        )(held, right_side, after)

    first_free, first_joined = near(0, first)
    second_free, second_joined = near(1, first_joined)
    first_free, second_free = move_by_core(first_free, 0, 0), move_by_core(second_free, 0, 1)
    first_joined = move_by_core(first_joined + got_second, 0, 0)
    second_joined = move_by_core(second_joined + got_first, 0, 1)
    own = pl.pallas_call(
        own_kernel,
        out_shape=[two] * 2,
        in_specs=[VMEM] * 2,
        out_specs=[VMEM] * 2,
        scratch_shapes=[total],
        compiler_params=params(36),
        cost_estimate=cost(1),
        name="own",
    )(held, right_side)
    keep, far, closest, after = pl.pallas_call(
        settle_kernel,
        out_shape=[jax.ShapeDtypeStruct((owned, width), F32)] * 4,
        in_specs=[VMEM] * 6,
        out_specs=[VMEM] * 4,
        compiler_params=params(16),
        name="settle",
    )(*own, first_free, first_joined, second_free, second_joined)
    return pl.pallas_call(
        gradient_kernel,
        out_shape=jax.ShapeDtypeStruct(kernel_coef.shape, F32),
        in_specs=[VMEM] * 8,
        out_specs=VMEM,
        compiler_params=params(16),
        name="gradient",
    )(
        keep, move_by_core(far, 1, 2), move_by_core(closest, 1, 0), move_by_core(after, 1, 1),
        kernel_coef, p_speed[None], s_speed[None], density[None],
    )


def solution(mesh):
    return jax.shard_map(
        per_device,
        mesh=mesh,
        in_specs=(
            P(None, ("row", "col"), None, None),
            P(("row", "col"), None, None, None),
            P(("row", "col"), None, None, None),
            P(),
            P(),
            P(),
            P(None, ("row", "col"), None),
            P(None, "row", "col"),
            P(None, ("row", "col")),
            P(("row", "col")),
            P(("row", "col")),
            P(("row", "col")),
        ),
        out_specs=P(None, ("row", "col")),
        check_vma=False,
    )
```
